32 devices in a mesh: geo: 4 (over x, core), curve: 8 (over z, y).
Axes of the slice: x: 2, y: 2, z: 4, core: 2. Of those that a mesh axis runs over, the one named last changes fastest.
Arguments:
- tokens: bfloat16 [32768, 512], P(('geo', 'curve')), parts along dimension 0, may hold values from -80 to 80
- w_query: bfloat16 [512, 512], replicated, may hold values from -0.25 to 0.25
- w_keyval: bfloat16 [512, 1024], replicated, may hold values from -0.25 to 0.25
- w_out: bfloat16 [512, 512], replicated, may hold values from -0.25 to 0.25
- block_list: int32 [256, 12], P(('geo', 'curve')), parts along dimension 0, may hold values from 0 to 63, as said below
- block_count: int32 [256], P(('geo', 'curve')), parts along dimension 0, may hold values from 2 to 12, as said below
- bnd_ids: int32 [2048], P('geo'), parts along dimension 0, may hold values from 0 to 8191, as said below
Outputs:
- mixed: bfloat16 [32768, 512], P(('geo', 'curve')), parts along dimension 0
The draws below stay inside these ranges and needn't reach their ends.
There are 4 independent parts, one for each index of `geo`. The reference program is written for one: setup_inputs(seed, part) draws one part's arguments, and reference() takes and returns one part's arrays. A program takes and returns all parts, laid end to end along the dimension named above; an argument that names none is the same for every part. Nothing has to cross between parts.
Inputs may be any that keep to these rules, and one draw needn't show every extreme that they name: `block_list`: entry 0 of row b is b itself; the other entries of a row are distinct blocks other than b whose owners lie at most two devices of curve away from b's owner (device index = block // 8); entries at or past block_count[b] are not used. `block_count`: it equals 12 on the first block of every device. `bnd_ids`: Distinct; listed in increasing order of owner id // 1024; exactly eight owners hold 128, 128, 96, 64, 48, 24, 16 and 8 of them, the other devices none.
All inputs are finite; a program needn't handle non-finite values.
Results may differ from the reference program's by a relative error of at most 0.012.
The reference program's roundings to bfloat16 on the way (of `queries`, `keyvals`, `weights` and `context`) count: a program that leaves them out, or rounds other values in their place, can miss the bound.
Values may be sent and summed in bfloat16 or wider, within the bound.
A program may use at most 128 MiB of HBM per device.

```python
import jax
import jax.numpy as jnp
from jax import lax

D = 512
HEADS = 8
BLOCK = 128
NB = 12
TOK_DEV = 1024
BCAP = 128
NBD = 512
TOKENS = 8192
N_CURVE = 8


def draw_tokens(key, part):
    base = jnp.clip(jax.random.normal(key, (TOKENS, D), jnp.float32), -5.5, 5.5)
    return base.astype(jnp.bfloat16)


def draw_block_list(key, part):
    nblk = TOKENS // BLOCK
    per_dev = TOK_DEV // BLOCK
    span = 5 * per_dev
    query = jnp.arange(nblk, dtype=jnp.int32)
    shard = query // per_dev
    low = jnp.maximum(shard - 2, 0) * per_dev
    high = jnp.minimum(shard + 3, N_CURVE) * per_dev
    cand = low[:, None] + jnp.arange(span, dtype=jnp.int32)[None, :]
    usable = (cand < high[:, None]) & (cand != query[:, None])
    noise = jax.random.randint(key, (nblk, span), 0, 1 << 20)
    score = jnp.where(usable, noise, 1 << 21) * 64 + jnp.arange(span, dtype=jnp.int32)[None, :]
    order = jnp.argsort(score, axis=1)
    chosen = jnp.take_along_axis(cand, order[:, :NB - 1], axis=1)
    return jnp.concatenate([query[:, None], chosen], axis=1).astype(jnp.int32)


def draw_block_count(key, part):
    nblk = TOKENS // BLOCK
    per_dev = TOK_DEV // BLOCK
    query = jnp.arange(nblk, dtype=jnp.int32)
    drawn = jax.random.randint(key, (nblk,), 2, NB + 1)
    return jnp.where(query % per_dev == 0, NB, drawn).astype(jnp.int32)


def draw_bnd_ids(key, part):
    inner = jax.random.fold_in(key, 77)
    owners = jax.random.permutation(jax.random.fold_in(inner, 1), N_CURVE)[:8]
    shares = jnp.array([16, 16, 12, 8, 6, 3, 2, 1], jnp.int32) * (BCAP // 16)
    counts = jnp.zeros((N_CURVE,), jnp.int32).at[owners].set(shares)
    shard_ids = jnp.arange(N_CURVE, dtype=jnp.int32)
    spots = jax.vmap(lambda r: jax.random.permutation(jax.random.fold_in(inner, 100 + r), TOK_DEV)[:BCAP])(shard_ids)
    glob = shard_ids[:, None] * TOK_DEV + spots.astype(jnp.int32)
    valid = jnp.arange(BCAP, dtype=jnp.int32)[None, :] < counts[:, None]
    flat = jnp.arange(N_CURVE * BCAP, dtype=jnp.int32).reshape(N_CURVE, BCAP)
    score = jnp.where(valid, flat, N_CURVE * BCAP + flat).reshape(-1)
    order = jnp.argsort(score)[:NBD]
    return glob.reshape(-1)[order].astype(jnp.int32)


def centred(rng, extent, spread, limit, held_as=jnp.bfloat16):
    entries = jax.random.normal(rng, extent, jnp.float32) * spread
    return jnp.minimum(jnp.maximum(entries, -limit), limit).astype(held_as)


def setup_inputs(seed: int = 0, part: int = 0) -> dict:
    streams_of = jax.random.split(jax.random.key(seed), 8)
    own_keys = jax.random.split(jax.random.fold_in(streams_of[7], part), 8)
    return {
        "tokens": draw_tokens(jax.random.fold_in(jax.random.fold_in(streams_of[7], part), 71), part),
        "w_query": centred(streams_of[1], (D, D), D ** -0.5, 0.25),
        "w_keyval": centred(streams_of[2], (D, 2 * D), D ** -0.5, 0.25),
        "w_out": centred(streams_of[3], (D, D), D ** -0.5, 0.25),
        "block_list": draw_block_list(jax.random.fold_in(jax.random.fold_in(streams_of[7], part), 71), part),
        "block_count": draw_block_count(jax.random.fold_in(jax.random.fold_in(streams_of[7], part), 71), part),
        "bnd_ids": draw_bnd_ids(jax.random.fold_in(jax.random.fold_in(streams_of[7], part), 71), part),
    }


def attend_group(query, keyvals_near, live, bnd_kv):
    width = D
    head_dim = D // HEADS
    groups = query.shape[0]
    scale = 1.0 / (head_dim ** 0.5)
    qh = query.reshape(groups, BLOCK, HEADS, head_dim).astype(jnp.float32)
    keys = keyvals_near[..., :width].reshape(groups, -1, HEADS, head_dim).astype(jnp.float32)
    vals = keyvals_near[..., width:].reshape(groups, -1, HEADS, head_dim).astype(jnp.float32)
    bkeys = bnd_kv[:, :width].reshape(-1, HEADS, head_dim).astype(jnp.float32)
    bvals = bnd_kv[:, width:].reshape(-1, HEADS, head_dim).astype(jnp.float32)
    near_scores = jnp.einsum('gqhd,gkhd->ghqk', qh, keys) * scale
    near_scores = jnp.where(live[:, None, None, :], near_scores, -1e30)
    far_scores = jnp.einsum('gqhd,khd->ghqk', qh, bkeys) * scale
    scores = jnp.concatenate([near_scores, far_scores], axis=-1)
    top = jnp.max(scores, axis=-1, keepdims=True)
    expo = jnp.exp(scores - top)
    weights = (expo / jnp.sum(expo, axis=-1, keepdims=True)).astype(jnp.bfloat16).astype(jnp.float32)
    span = keys.shape[1]
    ctx = jnp.einsum('ghqk,gkhd->gqhd', weights[..., :span], vals)
    ctx = ctx + jnp.einsum('ghqk,khd->gqhd', weights[..., span:], bvals)
    return ctx.reshape(groups * BLOCK, width).astype(jnp.bfloat16)


def reference(tokens, w_query, w_keyval, w_out, block_list, block_count, bnd_ids):
    queries = jnp.dot(tokens, w_query, preferred_element_type=jnp.float32).astype(jnp.bfloat16)
    keyvals = jnp.dot(tokens, w_keyval, preferred_element_type=jnp.float32).astype(jnp.bfloat16)
    bnd_kv = jnp.take(keyvals, bnd_ids.astype(jnp.int32), axis=0)
    nblk = TOKENS // BLOCK
    q_groups = queries.reshape(nblk // 2, 2, BLOCK, D)
    lists = block_list.astype(jnp.int32).reshape(nblk // 2, 2, NB)
    counts = block_count.astype(jnp.int32).reshape(nblk // 2, 2)

    def step(item):
        query, blocks, count = item
        rows = (blocks[:, :, None] * BLOCK + jnp.arange(BLOCK, dtype=jnp.int32)).reshape(2, NB * BLOCK)
        picked = jnp.take(keyvals, rows, axis=0)
        live = (jnp.arange(NB * BLOCK, dtype=jnp.int32) // BLOCK)[None, :] < count[:, None]
        return attend_group(query, picked, live, bnd_kv)

    context = lax.map(step, (q_groups, lists, counts)).reshape(TOKENS, D)
    return jnp.dot(context, w_out, preferred_element_type=jnp.float32).astype(jnp.bfloat16)
```

```python
import functools

import jax
import jax.numpy as jnp
from jax import lax
from jax.experimental import pallas as pl
from jax.experimental.pallas import tpu as pltpu
from jax.sharding import PartitionSpec as P

HEADS = 8
BLOCK = 128
NB = 12
BCAP = 128
LOW = -1e30
ROWS = 256

FIRST, BOUND, MIDDLE, LAST = range(4)


def cast_dot(a, b, dims):
    out = lax.dot_general(a, b, (dims, ((), ())), preferred_element_type=jnp.float32)
    return out.astype(jnp.bfloat16)


def project(tok, wk, wvt, k_ref, vt_ref, base):
    @pl.loop(0, tok.shape[0] // ROWS)
    def _(t):
        rows = tok[pl.ds(pl.multiple_of(t * ROWS, ROWS), ROWS), :]
        k = cast_dot(rows, wk[...], ((1,), (0,)))
        vt = cast_dot(wvt[...], rows, ((1,), (1,)))
        for i in range(ROWS // BLOCK):
            at = base + t * (ROWS // BLOCK) + i
            k_ref[at] = k[i * BLOCK:(i + 1) * BLOCK, :]
            vt_ref[at] = vt[:, i * BLOCK:(i + 1) * BLOCK]


def local_source(kind, slot, me):
    near = 3 - 2 * lax.rem(me, 2)
    if kind == FIRST:
        return jnp.where(slot == 2, 0, -1)
    if kind == MIDDLE:
        return jnp.where(slot == 0, 0, jnp.where(slot == 4, 1, jnp.where(slot == near, 2, -1)))
    return jnp.where(slot == 4 - near, 0, -1)


def compact(kind, qb, me, nblocks, lists, counts, idx):
    used = counts[qb]
    n = jnp.int32(0)
    for i in range(NB):
        rel = jnp.clip(lists[qb, i] - (me - 2) * nblocks, 0, 5 * nblocks - 1)
        slot = lax.div(rel, nblocks)
        src = local_source(kind, slot, me)
        take = jnp.logical_and(i < used, src >= 0)
        idx[n] = jnp.where(take, src * nblocks + rel - slot * nblocks, 0)
        n = n + take.astype(jnp.int32)
    idx[n] = 0
    return n


def update(k, v, q, bias, acc, m_ref, l_ref, row):
    keys = k.shape[0]
    s = jnp.dot(k, q, preferred_element_type=jnp.float32)
    if bias is not None:
        s = jnp.concatenate([s[:BLOCK], s[BLOCK:] + bias], axis=0)
    m_old = m_ref[row]
    m_new = jnp.maximum(m_old, jnp.max(s, axis=0, keepdims=True))
    p = jnp.exp(s - m_new).astype(jnp.bfloat16)
    alpha = jnp.exp(m_old - m_new)
    va = jnp.concatenate([v, jnp.ones((16, keys), jnp.bfloat16)], axis=0)
    pv = jnp.dot(va, p, preferred_element_type=jnp.float32)
    acc[row, :64, :] = acc[row, :64, :] * alpha[:, :BLOCK] + pv[:64, :BLOCK]
    acc[row, 64:, :] = acc[row, 64:, :] * alpha[:, BLOCK:] + pv[64:128, BLOCK:]
    l_ref[row] = l_ref[row] * alpha + pv[128:129, :]
    m_ref[row] = m_new


def phase(kind, nsrc, *refs):
    refs = list(refs)
    take = lambda n: [refs.pop(0) for _ in range(n)]
    toks = take(nsrc)
    wk, wvt = take(2)
    if kind != BOUND:
        me_ref, lists, counts = take(3)
    if kind == FIRST:
        (wqt,) = take(1)
    else:
        qt_in, acc_in, m_in, l_in = take(4)
    if kind == LAST:
        wo, out = take(2)
        acc, m_ref, l_ref = take(3)
    else:
        if kind == FIRST:
            (qt_out,) = take(1)
        acc, m_ref, l_ref = take(3)
    k_ref, vt_ref, qbd = take(3)
    if kind != BOUND:
        (idx,) = take(1)
        me = me_ref[0]
    qt_ref = qt_out if kind == FIRST else qt_in
    nqb, width = qt_ref.shape[0], qt_ref.shape[1]
    pairs = width // BLOCK

    if kind == FIRST:
        @pl.loop(0, toks[0].shape[0] // ROWS)
        def _(t):
            rows = toks[0][pl.ds(pl.multiple_of(t * ROWS, ROWS), ROWS), :]
            q = lax.dot_general(wqt[...], rows, (((1,), (1,)), ((), ())), preferred_element_type=jnp.float32)
            q = q.astype(jnp.bfloat16) * jnp.bfloat16(0.125)
            for i in range(ROWS // BLOCK):
                qt_ref[t * (ROWS // BLOCK) + i] = q[:, i * BLOCK:(i + 1) * BLOCK]

    for s, tok in enumerate(toks):
        project(tok, wk, wvt, k_ref, vt_ref, s * (tok.shape[0] // BLOCK))

    @pl.loop(0, nqb)
    def _(qb):
        zero = jnp.zeros((64, BLOCK), jnp.bfloat16)
        for hp in range(pairs):
            q0 = qt_ref[qb, hp * BLOCK:hp * BLOCK + 64, :]
            q1 = qt_ref[qb, hp * BLOCK + 64:(hp + 1) * BLOCK, :]
            qbd[hp, :64, :] = jnp.concatenate([q0, zero], axis=1)
            qbd[hp, 64:, :] = jnp.concatenate([zero, q1], axis=1)
            row = qb * pairs + hp
            if kind == FIRST:
                acc[row] = jnp.zeros_like(acc[row])
                m_ref[row] = jnp.full_like(m_ref[row], LOW)
                l_ref[row] = jnp.zeros_like(l_ref[row])
            else:
                acc[row] = acc_in[row]
                m_ref[row] = m_in[row]
                l_ref[row] = l_in[row]
        if kind == BOUND:
            nb = k_ref.shape[0]
            for hp in range(pairs):
                cut = slice(hp * BLOCK, (hp + 1) * BLOCK)
                k = jnp.concatenate([k_ref[j, :, cut] for j in range(nb)], axis=0)
                v = jnp.concatenate([vt_ref[j, cut, :] for j in range(nb)], axis=1)
                update(k, v, qbd[hp], None, acc, m_ref, l_ref, qb * pairs + hp)
        else:
            n = compact(kind, qb, me, nqb, lists, counts, idx)

            def step(j, carry):
                b0, b1 = idx[2 * j], idx[2 * j + 1]
                bias = jnp.where(2 * j + 1 < n, 0.0, LOW).astype(jnp.float32)
                for hp in range(pairs):
                    cut = slice(hp * BLOCK, (hp + 1) * BLOCK)
                    k = jnp.concatenate([k_ref[b0, :, cut], k_ref[b1, :, cut]], axis=0)
                    v = jnp.concatenate([vt_ref[b0, cut, :], vt_ref[b1, cut, :]], axis=1)
                    update(k, v, qbd[hp], bias, acc, m_ref, l_ref, qb * pairs + hp)
                return carry

            lax.fori_loop(0, lax.div(n + 1, 2), step, 0)
        if kind == LAST:
            parts = []
            for hp in range(pairs):
                row = qb * pairs + hp
                inv = 1.0 / l_ref[row]
                parts.append(acc[row, :64, :] * inv[:, :BLOCK])
                parts.append(acc[row, 64:, :] * inv[:, BLOCK:])
            ctx = jnp.concatenate(parts, axis=0).T.astype(jnp.bfloat16)
            out[pl.ds(pl.multiple_of(qb * BLOCK, BLOCK), BLOCK), :] = cast_dot(ctx, wo[...], ((1,), (0,)))


def run_phase(kind, toks, wk, wvt, lists=None, wqt=None, state=None, wo=None):
    width = wk.shape[0]
    pairs = width // BLOCK
    nkb = sum(t.shape[0] for t in toks) // BLOCK
    vmem, smem = pl.BlockSpec(memory_space=pltpu.VMEM), pl.BlockSpec(memory_space=pltpu.SMEM)
    args = list(toks) + [wk, wvt]
    specs = [vmem] * len(args)
    if kind != BOUND:
        args += list(lists)
        specs += [smem] * 3
    if kind == FIRST:
        args.append(wqt)
        nqb = toks[0].shape[0] // BLOCK
    else:
        args += list(state)
        nqb = state[0].shape[0]
    if kind == LAST:
        args.append(wo)
    specs += [vmem] * (len(args) - len(specs))
    sums = [(nqb * pairs, BLOCK, BLOCK), (nqb * pairs, 1, 2 * BLOCK), (nqb * pairs, 1, 2 * BLOCK)]
    scratch = []
    if kind == LAST:
        outs = [jax.ShapeDtypeStruct((nqb * BLOCK, width), jnp.bfloat16)]
        scratch += [pltpu.VMEM(s, jnp.float32) for s in sums]
    else:
        outs = [jax.ShapeDtypeStruct(s, jnp.float32) for s in sums]
        if kind == FIRST:
            outs = [jax.ShapeDtypeStruct((nqb, width, BLOCK), jnp.bfloat16)] + outs
    scratch += [
        pltpu.VMEM((nkb, BLOCK, width), jnp.bfloat16),
        pltpu.VMEM((nkb, width, BLOCK), jnp.bfloat16),
        pltpu.VMEM((pairs, BLOCK, 2 * BLOCK), jnp.bfloat16),
    ]
    if kind != BOUND:
        scratch.append(pltpu.SMEM((16,), jnp.int32))
    units = {FIRST: 18, BOUND: 32, MIDDLE: 34, LAST: 11}[kind]
    cost = pl.CostEstimate(
        flops=units * 8 * 2 * BLOCK ** 3 * 8 + nkb * BLOCK * width * width * 4,
        bytes_accessed=8 << 20,
        transcendentals=units * 8 * BLOCK * BLOCK,
    )
    return pl.pallas_call(
        functools.partial(phase, kind, len(toks)),
        out_shape=outs,
        in_specs=specs,
        out_specs=[vmem] * len(outs),
        scratch_shapes=scratch,
        compiler_params=pltpu.CompilerParams(vmem_limit_bytes=40 << 20),
        cost_estimate=cost,
        name=("attend_own", "attend_bound", "attend_middle", "attend_last")[kind],
    )(*args)


def send(value, pairs):
    return lax.ppermute(value, "curve", pairs)


def on_device(tokens, w_query, w_keyval, w_out, block_list, block_count, bnd_ids):
    tok_dev, width = tokens.shape
    nbound = bnd_ids.shape[0]
    size = lax.axis_size("curve")
    member = lax.axis_index("curve")
    everyone = range(size)

    owner = bnd_ids // tok_dev
    slots = jnp.arange(BCAP, dtype=jnp.int32)
    my_start = jnp.sum((owner < member).astype(jnp.int32))
    padded_ids = jnp.concatenate([bnd_ids, jnp.zeros((BCAP,), jnp.int32)])
    my_ids = lax.dynamic_slice_in_dim(padded_ids, my_start, BCAP) - member * tok_dev
    pick = (my_ids[:, None] == jnp.arange(tok_dev, dtype=jnp.int32)[None, :]).astype(jnp.bfloat16)
    rows = jnp.dot(pick, tokens, preferred_element_type=jnp.float32).astype(jnp.bfloat16)
    gathered = lax.all_gather(rows, "curve", axis=0, tiled=True)

    from_two_behind = send(tokens, [(i, i + 2) for i in everyone if i + 2 < size])
    from_two_ahead = send(tokens, [(i, i - 2) for i in everyone if i >= 2])
    mate = send(tokens, [(i, i ^ 1) for i in everyone])
    half = tok_dev // 2
    relay = jnp.where(member % 2 == 0, from_two_ahead[:half], from_two_behind[:half])
    low = send(relay, [(i, i ^ 1) for i in everyone])
    hops = [(i, i + 2 - 4 * (i % 2)) for i in everyone]
    high = send(mate[half:], [(a, b) for a, b in hops if 0 <= b < size])

    wk = w_keyval[:, :width]
    wvt = w_keyval[:, width:].T
    lists = (member.reshape(1).astype(jnp.int32), block_list, block_count)

    qt, *sums = run_phase(FIRST, [tokens], wk, wvt, lists=lists, wqt=w_query.T)

    slot_range = jnp.arange(nbound, dtype=jnp.int32)
    owner_start = jnp.sum((owner[None, :] < owner[:, None]).astype(jnp.int32), axis=1)
    source = owner * BCAP + slot_range - owner_start
    choose = (source[:, None] == jnp.arange(size * BCAP, dtype=jnp.int32)[None, :]).astype(jnp.bfloat16)
    bound = jnp.dot(choose, gathered, preferred_element_type=jnp.float32).astype(jnp.bfloat16)
    sums = run_phase(BOUND, [bound], wk, wvt, state=[qt] + list(sums))
    sums = run_phase(
        MIDDLE, [from_two_behind, from_two_ahead, mate], wk, wvt, lists=lists, state=[qt] + list(sums)
    )
    far = jnp.concatenate([low, high], axis=0)
    (mixed,) = run_phase(LAST, [far], wk, wvt, lists=lists, state=[qt] + list(sums), wo=w_out)
    return mixed


def solution(mesh):
    in_specs = (
        P(("geo", "curve"), None),
        P(),
        P(),
        P(),
        P(("geo", "curve"), None),
        P(("geo", "curve")),
        P("geo"),
    )
    out_specs = P(("geo", "curve"), None)
    return jax.shard_map(
        on_device, mesh=mesh, in_specs=in_specs, out_specs=out_specs, check_vma=False
    )
```

```python
import functools

import jax
import jax.numpy as jnp
from jax import lax
from jax.experimental import pallas as pl
from jax.experimental.pallas import tpu as pltpu
from jax.sharding import PartitionSpec as P

HEADS = 8
BLOCK = 128
NB = 12
BCAP = 128
LOW = -1e30
ROWS = 256

FIRST, BOUND, MIDDLE, LAST = range(4)


def cast_dot(a, b, dims):
    out = lax.dot_general(a, b, (dims, ((), ())), preferred_element_type=jnp.float32)
    return out.astype(jnp.bfloat16)


def project(tok, wk, wvt, k_ref, vt_ref, norm_ref, base):
    width = wk.shape[0]
    feature = lax.broadcasted_iota(jnp.int32, (width, BLOCK), 0)
    head = lax.broadcasted_iota(jnp.int32, (width, BLOCK), 1)
    ind = jnp.where(feature >> 6 == head, 1.0, 0.0).astype(jnp.bfloat16)

    @pl.loop(0, tok.shape[0] // ROWS)
    def _(t):
        rows = tok[pl.ds(pl.multiple_of(t * ROWS, ROWS), ROWS), :]
        k = cast_dot(rows, wk[...], ((1,), (0,)))
        vt = cast_dot(wvt[...], rows, ((1,), (1,)))
        for i in range(ROWS // BLOCK):
            at = base + t * (ROWS // BLOCK) + i
            k_ref[at] = k[i * BLOCK:(i + 1) * BLOCK, :]
            vt_ref[at] = vt[:, i * BLOCK:(i + 1) * BLOCK]
        norm = jnp.dot(k * k, ind, preferred_element_type=jnp.float32)
        norm_ref[...] = jnp.maximum(norm_ref[...], jnp.max(norm, axis=0, keepdims=True))


def local_source(kind, slot, me):
    near = 3 - 2 * lax.rem(me, 2)
    if kind == FIRST:
        return jnp.where(slot == 2, 0, -1)
    if kind == MIDDLE:
        return jnp.where(slot == 0, 0, jnp.where(slot == 4, 1, jnp.where(slot == near, 2, -1)))
    return jnp.where(slot == 4 - near, 0, -1)


def make_plans(me, nqb, nbound, lists, counts, plan, plan_qb, plan_n):
    for kind in (FIRST, MIDDLE, LAST):
        def row(qb, at):
            def entry(i, n):
                rel = jnp.clip(lists[qb, i] - (me - 2) * nqb, 0, 5 * nqb - 1)
                slot = lax.div(rel, nqb)
                src = local_source(kind, slot, me)
                take = jnp.logical_and(i < counts[qb], src >= 0)
                plan[kind, n] = jnp.where(take, src * nqb + rel - slot * nqb, -1)
                return n + take.astype(jnp.int32)

            n = lax.fori_loop(0, NB, entry, at)
            plan[kind, n] = -1
            top = at + 2 * lax.div(n - at + 1, 2)

            @pl.loop(lax.div(at, 2), lax.div(top, 2))
            def _(j):
                plan_qb[kind, j] = qb
            return top

        top = lax.fori_loop(0, nqb, row, jnp.int32(0))
        plan[kind, top] = -1
        plan[kind, top + 1] = -1
        plan_qb[kind, lax.div(top, 2)] = 0
        plan_n[kind] = lax.div(top + 2, 4)
    each = nbound // BLOCK // 2

    @pl.loop(0, nqb * each)
    def _(j):
        plan[BOUND, 2 * j] = 2 * lax.rem(j, each)
        plan[BOUND, 2 * j + 1] = 2 * lax.rem(j, each) + 1
        plan_qb[BOUND, j] = lax.div(j, each)
    plan_n[BOUND] = nqb * each // 2


def phase(kind, nsrc, nbound, *refs):
    refs = list(refs)
    take = lambda n: [refs.pop(0) for _ in range(n)]
    toks = take(nsrc)
    wk, wvt = take(2)
    if kind == FIRST:
        me_ref, lists, counts, wqt = take(4)
    else:
        plan, plan_qb, plan_n, fast_in, qn_in, qbd, acc_in, m_in, l_in = take(9)
    if kind == LAST:
        wo, out = take(2)
    else:
        if kind == FIRST:
            plan, plan_qb, plan_n, qn_out, qbd = take(5)
        (fast_out,) = take(1)
    acc, m_ref, l_ref, k_ref, vt_ref, p_ref, norm_ref = take(7)
    nqb, pairs = qbd.shape[0], qbd.shape[1]

    norm_ref[...] = jnp.zeros_like(norm_ref)
    if kind == FIRST:
        (qn_ref,) = take(1)
        make_plans(me_ref[0], nqb, nbound, lists, counts, plan, plan_qb, plan_n)
        qn_ref[...] = jnp.zeros_like(qn_ref)
        zero = jnp.zeros((64, BLOCK), jnp.bfloat16)

        @pl.loop(0, toks[0].shape[0] // ROWS)
        def _(t):
            rows = toks[0][pl.ds(pl.multiple_of(t * ROWS, ROWS), ROWS), :]
            q = lax.dot_general(wqt[...], rows, (((1,), (1,)), ((), ())), preferred_element_type=jnp.float32)
            q = q.astype(jnp.bfloat16) * jnp.bfloat16(0.125)
            for i in range(ROWS // BLOCK):
                for hp in range(pairs):
                    cut = q[hp * BLOCK:(hp + 1) * BLOCK, i * BLOCK:(i + 1) * BLOCK]
                    at = t * (ROWS // BLOCK) + i
                    qbd[at, hp, :64, :] = jnp.concatenate([cut[:64], zero], axis=1)
                    qbd[at, hp, 64:, :] = jnp.concatenate([zero, cut[64:]], axis=1)
            q = q.astype(jnp.float32)
            for h in range(2 * pairs):
                part = q[h * 64:(h + 1) * 64, :]
                qn_ref[...] = jnp.maximum(qn_ref[...], jnp.sum(part * part, axis=0, keepdims=True))

        acc[...] = jnp.zeros_like(acc)
        l_ref[...] = jnp.zeros_like(l_ref)
        qn = jnp.max(qn_ref[...])
        qn_out[0] = qn
    else:
        acc[...] = acc_in[...]
        l_ref[...] = l_in[...]
        m_ref[...] = m_in[...]
        qn = qn_in[0]

    for s, tok in enumerate(toks):
        project(tok, wk, wvt, k_ref, vt_ref, norm_ref, s * (tok.shape[0] // BLOCK))
    small = qn * jnp.max(norm_ref[...]) <= 3600.0
    fast = small if kind == FIRST else jnp.logical_and(small, fast_in[0] == 1)
    if kind == FIRST:
        m_ref[...] = jnp.full_like(m_ref, jnp.where(fast, 0.0, LOW))
    if kind != LAST:
        fast_out[0] = fast.astype(jnp.int32)
    count = plan_n[kind]

    def blocks(item):
        return jnp.maximum(plan[kind, 2 * item], 0), jnp.maximum(plan[kind, 2 * item + 1], 0)

    def scores(item):
        b0, b1 = blocks(item)
        bias0 = jnp.where(plan[kind, 2 * item] < 0, LOW, 0.0).astype(jnp.float32)
        bias1 = jnp.where(plan[kind, 2 * item + 1] < 0, LOW, 0.0).astype(jnp.float32)
        qb = plan_qb[kind, item]
        made = []
        for hp in range(pairs):
            cut = slice(hp * BLOCK, (hp + 1) * BLOCK)
            k = jnp.concatenate([k_ref[b0, :, cut], k_ref[b1, :, cut]], axis=0)
            s = jnp.dot(k, qbd[qb, hp], preferred_element_type=jnp.float32)
            made.append((s[:BLOCK] + bias0, s[BLOCK:] + bias1))
        return made

    def values(item, hp):
        b0, b1 = blocks(item)
        cut = slice(hp * BLOCK, (hp + 1) * BLOCK)
        v = jnp.concatenate([vt_ref[b0, cut, :], vt_ref[b1, cut, :]], axis=1)
        return jnp.concatenate([v, jnp.ones((16, 2 * BLOCK), jnp.bfloat16)], axis=0)

    @pl.when(fast)
    def _():
        def weigh(item, slot):
            for hp, halves in enumerate(scores(item)):
                for i, s in enumerate(halves):
                    p_ref[slot, hp, i * BLOCK:(i + 1) * BLOCK, :] = jnp.exp(s).astype(jnp.bfloat16)

        def gather(item, slot):
            qb = plan_qb[kind, item]
            pvs = [
                jnp.dot(values(item, hp), p_ref[slot, hp], preferred_element_type=jnp.float32)
                for hp in range(pairs)
            ]
            for hp, pv in enumerate(pvs):
                row = qb * pairs + hp
                acc[row, :64, :] = acc[row, :64, :] + pv[:64, :BLOCK]
                acc[row, 64:, :] = acc[row, 64:, :] + pv[64:BLOCK, BLOCK:]
                l_ref[row] = l_ref[row] + pv[BLOCK:BLOCK + 1, :]

        p_ref[1] = jnp.zeros_like(p_ref[1])

        def two(t, carry):
            gather(jnp.maximum(2 * t - 1, 0), 1)
            weigh(2 * t, 0)
            gather(2 * t, 0)
            weigh(2 * t + 1, 1)
            return carry

        lax.fori_loop(0, count, two, 0)
        gather(jnp.maximum(2 * count - 1, 0), 1)

    @pl.when(jnp.logical_not(fast))
    def _():
        def one(item, carry):
            qb = plan_qb[kind, item]
            for hp, halves in enumerate(scores(item)):
                row = qb * pairs + hp
                s = jnp.concatenate(halves, axis=0)
                m_old = m_ref[row]
                m_new = jnp.maximum(m_old, jnp.max(s, axis=0, keepdims=True))
                p = jnp.exp(s - m_new).astype(jnp.bfloat16)
                alpha = jnp.exp(m_old - m_new)
                pv = jnp.dot(values(item, hp), p, preferred_element_type=jnp.float32)
                acc[row, :64, :] = acc[row, :64, :] * alpha[:, :BLOCK] + pv[:64, :BLOCK]
                acc[row, 64:, :] = acc[row, 64:, :] * alpha[:, BLOCK:] + pv[64:BLOCK, BLOCK:]
                l_ref[row] = l_ref[row] * alpha + pv[BLOCK:BLOCK + 1, :]
                m_ref[row] = m_new
            return carry

        lax.fori_loop(0, 2 * count, one, 0)

    if kind == LAST:
        @pl.loop(0, nqb)
        def _(qb):
            parts = []
            for hp in range(pairs):
                row = qb * pairs + hp
                inv = 1.0 / l_ref[row]
                parts.append(acc[row, :64, :] * inv[:, :BLOCK])
                parts.append(acc[row, 64:, :] * inv[:, BLOCK:])
            ctx = jnp.concatenate(parts, axis=0).T.astype(jnp.bfloat16)
            out[pl.ds(pl.multiple_of(qb * BLOCK, BLOCK), BLOCK), :] = cast_dot(ctx, wo[...], ((1,), (0,)))


def run_phase(kind, toks, wk, wvt, nbound, lists=None, wqt=None, state=None, wo=None):
    width = wk.shape[0]
    pairs = width // BLOCK
    nkb = sum(t.shape[0] for t in toks) // BLOCK
    vmem, smem = pl.BlockSpec(memory_space=pltpu.VMEM), pl.BlockSpec(memory_space=pltpu.SMEM)
    args, specs = list(toks) + [wk, wvt], [vmem] * (len(toks) + 2)
    if kind == FIRST:
        args += list(lists) + [wqt]
        specs += [smem] * 3 + [vmem]
        nqb = toks[0].shape[0] // BLOCK
    else:
        args += list(state)
        specs += [smem] * 5 + [vmem] * 4
        nqb = state[5].shape[0]
    if kind == LAST:
        args.append(wo)
        specs.append(vmem)
    sums = [(nqb * pairs, BLOCK, BLOCK), (nqb * pairs, 1, 2 * BLOCK), (nqb * pairs, 1, 2 * BLOCK)]
    outs, out_specs, scratch = [], [], []
    if kind == LAST:
        outs.append(jax.ShapeDtypeStruct((nqb * BLOCK, width), jnp.bfloat16))
        out_specs.append(vmem)
        scratch += [pltpu.VMEM(s, jnp.float32) for s in sums]
    else:
        if kind == FIRST:
            room = nqb * NB + 16
            outs += [
                jax.ShapeDtypeStruct((4, room), jnp.int32),
                jax.ShapeDtypeStruct((4, room), jnp.int32),
                jax.ShapeDtypeStruct((4,), jnp.int32),
                jax.ShapeDtypeStruct((1,), jnp.float32),
                jax.ShapeDtypeStruct((nqb, pairs, BLOCK, 2 * BLOCK), jnp.bfloat16),
            ]
            out_specs += [smem] * 4 + [vmem]
        outs.append(jax.ShapeDtypeStruct((1,), jnp.int32))
        out_specs.append(smem)
        outs += [jax.ShapeDtypeStruct(s, jnp.float32) for s in sums]
        out_specs += [vmem] * 3
    scratch += [
        pltpu.VMEM((nkb, BLOCK, width), jnp.bfloat16),
        pltpu.VMEM((nkb, width, BLOCK), jnp.bfloat16),
        pltpu.VMEM((2, pairs, 2 * BLOCK, 2 * BLOCK), jnp.bfloat16),
        pltpu.VMEM((1, BLOCK), jnp.float32),
    ]
    if kind == FIRST:
        scratch.append(pltpu.VMEM((1, ROWS), jnp.float32))
    units = {FIRST: 18, BOUND: 32, MIDDLE: 34, LAST: 11}[kind]
    cost = pl.CostEstimate(
        flops=units * 8 * 2 * BLOCK ** 3 * 8 + nkb * BLOCK * width * width * 4,
        bytes_accessed=8 << 20,
        transcendentals=units * 8 * BLOCK * BLOCK,
    )
    return pl.pallas_call(
        functools.partial(phase, kind, len(toks), nbound),
        out_shape=outs,
        in_specs=specs,
        out_specs=out_specs,
        scratch_shapes=scratch,
        compiler_params=pltpu.CompilerParams(vmem_limit_bytes=40 << 20),
        cost_estimate=cost,
        name=("attend_own", "attend_bound", "attend_middle", "attend_last")[kind],
    )(*args)


def send(value, pairs):
    return lax.ppermute(value, "curve", pairs)


def on_device(tokens, w_query, w_keyval, w_out, block_list, block_count, bnd_ids):
    tok_dev, width = tokens.shape
    nbound = bnd_ids.shape[0]
    size = lax.axis_size("curve")
    member = lax.axis_index("curve")
    everyone = range(size)

    owner = bnd_ids // tok_dev
    slots = jnp.arange(BCAP, dtype=jnp.int32)
    my_start = jnp.sum((owner < member).astype(jnp.int32))
    padded_ids = jnp.concatenate([bnd_ids, jnp.zeros((BCAP,), jnp.int32)])
    my_ids = lax.dynamic_slice_in_dim(padded_ids, my_start, BCAP) - member * tok_dev
    pick = (my_ids[:, None] == jnp.arange(tok_dev, dtype=jnp.int32)[None, :]).astype(jnp.bfloat16)
    rows = jnp.dot(pick, tokens, preferred_element_type=jnp.float32).astype(jnp.bfloat16)
    gathered = lax.all_gather(rows, "curve", axis=0, tiled=True)

    from_two_behind = send(tokens, [(i, i + 2) for i in everyone if i + 2 < size])
    from_two_ahead = send(tokens, [(i, i - 2) for i in everyone if i >= 2])
    mate = send(tokens, [(i, i ^ 1) for i in everyone])

    wk = w_keyval[:, :width]
    wvt = w_keyval[:, width:].T
    lists = (member.reshape(1).astype(jnp.int32), block_list, block_count)
    *plan, qn, qbd, fast, acc, top, total = run_phase(
        FIRST, [tokens], wk, wvt, nbound, lists=lists, wqt=w_query.T
    )

    slot_range = jnp.arange(nbound, dtype=jnp.int32)
    owner_start = jnp.sum((owner[None, :] < owner[:, None]).astype(jnp.int32), axis=1)
    source = owner * BCAP + slot_range - owner_start
    choose = (source[:, None] == jnp.arange(size * BCAP, dtype=jnp.int32)[None, :]).astype(jnp.bfloat16)
    bound = jnp.dot(choose, gathered, preferred_element_type=jnp.float32).astype(jnp.bfloat16)
    fast, acc, top, total = run_phase(
        BOUND, [bound], wk, wvt, nbound, state=[*plan, fast, qn, qbd, acc, top, total]
    )

    after = jnp.minimum(fast[0], 0)
    half = tok_dev // 2
    relay = jnp.where(member % 2 == after, from_two_ahead[:half], from_two_behind[:half])
    low = send(relay, [(i, i ^ 1) for i in everyone])
    hops = [(i, i + 2 - 4 * (i % 2)) for i in everyone]
    upper = lax.dynamic_slice_in_dim(mate, half + after, half)
    high = send(upper, [(a, b) for a, b in hops if 0 <= b < size])

    fast, acc, top, total = run_phase(
        MIDDLE,
        [from_two_behind, from_two_ahead, mate],
        wk,
        wvt,
        nbound,
        state=[*plan, fast, qn, qbd, acc, top, total],
    )
    far = jnp.concatenate([low, high], axis=0)
    (mixed,) = run_phase(
        LAST, [far], wk, wvt, nbound, state=[*plan, fast, qn, qbd, acc, top, total], wo=w_out
    )
    return mixed


def solution(mesh):
    in_specs = (
        P(("geo", "curve"), None),
        P(),
        P(),
        P(),
        P(("geo", "curve"), None),
        P(("geo", "curve")),
        P("geo"),
    )
    out_specs = P(("geo", "curve"), None)
    return jax.shard_map(
        on_device, mesh=mesh, in_specs=in_specs, out_specs=out_specs, check_vma=False
    )
```

```python
import functools

import jax
import jax.numpy as jnp
from jax import lax
from jax.experimental import pallas as pl
from jax.experimental.pallas import tpu as pltpu
from jax.sharding import PartitionSpec as P

HEADS = 8
BLOCK = 128
NB = 12
BCAP = 128
LOW = -1e30
ROWS = 256

FIRST, MIDDLE, LAST = range(3)
PLAN_LEN = 128


def cast_dot(a, b, dims):
    out = lax.dot_general(a, b, (dims, ((), ())), preferred_element_type=jnp.float32)
    return out.astype(jnp.bfloat16)


def project(tok, wk, wvt, k_ref, vt_ref, norm_ref, base):
    width = wk.shape[0]
    feature = lax.broadcasted_iota(jnp.int32, (width, BLOCK), 0)
    head = lax.broadcasted_iota(jnp.int32, (width, BLOCK), 1)
    ind = jnp.where(feature >> 6 == head, 1.0, 0.0).astype(jnp.bfloat16)

    @pl.loop(0, tok.shape[0] // ROWS)
    def _(t):
        rows = tok[pl.ds(pl.multiple_of(t * ROWS, ROWS), ROWS), :]
        k = cast_dot(rows, wk[...], ((1,), (0,)))
        vt = cast_dot(wvt[...], rows, ((1,), (1,)))
        for i in range(ROWS // BLOCK):
            at = base + t * (ROWS // BLOCK) + i
            k_ref[at] = k[i * BLOCK:(i + 1) * BLOCK, :]
            vt_ref[at] = vt[:, i * BLOCK:(i + 1) * BLOCK]
        norm = jnp.dot(k * k, ind, preferred_element_type=jnp.float32)
        norm_ref[...] = jnp.maximum(norm_ref[...], jnp.max(norm, axis=0, keepdims=True))


def local_source(kind, slot, me):
    near = 3 - 2 * lax.rem(me, 2)
    if kind == FIRST:
        return jnp.where(slot == 2, 0, -1)
    if kind == MIDDLE:
        return jnp.where(slot == 0, 0, jnp.where(slot == 4, 1, jnp.where(slot == near, 2, -1)))
    return jnp.where(slot == 4 - near, 0, -1)


def make_plans(me, nqb, nbound, lists, counts, plan):
    for kind in (FIRST, MIDDLE, LAST):
        def row(qb, at):
            def entry(i, n):
                rel = jnp.clip(lists[qb, i] - (me - 2) * nqb, 0, 5 * nqb - 1)
                slot = lax.div(rel, nqb)
                src = local_source(kind, slot, me)
                take = jnp.logical_and(i < counts[qb], src >= 0)
                plan[kind, n] = jnp.where(take, src * nqb + rel - slot * nqb, -1)
                return n + take.astype(jnp.int32)

            n = lax.fori_loop(0, NB, entry, at)
            plan[kind, n] = -1
            top = at + 2 * lax.div(n - at + 1, 2)
            if kind == LAST:
                for j in range(nbound // BLOCK):
                    plan[kind, top + j] = nqb + j
                top = top + nbound // BLOCK

            @pl.loop(lax.div(at, 2), lax.div(top, 2))
            def _(j):
                plan[4 + kind, j] = qb
            return top

        top = lax.fori_loop(0, nqb, row, jnp.int32(0))
        plan[kind, top] = -1
        plan[kind, top + 1] = -1
        plan[4 + kind, lax.div(top, 2)] = 0
        plan[7, kind] = lax.div(top + 2, 4)


def phase(kind, nsrc, nbound, *refs):
    refs = list(refs)
    take = lambda n: [refs.pop(0) for _ in range(n)]
    toks = take(nsrc)
    wk, wvt = take(2)
    if kind == FIRST:
        me_ref, lists, counts, wqt = take(4)
    else:
        plan, qbd, acc_in, m_in, l_in = take(5)
    if kind == LAST:
        wo, out = take(2)
    elif kind == FIRST:
        plan, qbd = take(2)
    acc, m_ref, l_ref, k_ref, vt_ref, p_ref, norm_ref = take(7)
    nqb, pairs = qbd.shape[0], qbd.shape[1]

    norm_ref[...] = jnp.zeros_like(norm_ref)
    if kind == FIRST:
        (qn_ref,) = take(1)
        make_plans(me_ref[0], nqb, nbound, lists, counts, plan)
        qn_ref[...] = jnp.zeros_like(qn_ref)
        zero = jnp.zeros((64, BLOCK), jnp.bfloat16)

        @pl.loop(0, toks[0].shape[0] // ROWS)
        def _(t):
            rows = toks[0][pl.ds(pl.multiple_of(t * ROWS, ROWS), ROWS), :]
            q = lax.dot_general(wqt[...], rows, (((1,), (1,)), ((), ())), preferred_element_type=jnp.float32)
            q = q.astype(jnp.bfloat16) * jnp.bfloat16(0.125)
            for i in range(ROWS // BLOCK):
                for hp in range(pairs):
                    cut = q[hp * BLOCK:(hp + 1) * BLOCK, i * BLOCK:(i + 1) * BLOCK]
                    at = t * (ROWS // BLOCK) + i
                    qbd[at, hp, :64, :] = jnp.concatenate([cut[:64], zero], axis=1)
                    qbd[at, hp, 64:, :] = jnp.concatenate([zero, cut[64:]], axis=1)
            q = q.astype(jnp.float32)
            for h in range(2 * pairs):
                part = q[h * 64:(h + 1) * 64, :]
                qn_ref[...] = jnp.maximum(qn_ref[...], jnp.sum(part * part, axis=0, keepdims=True))

        acc[...] = jnp.zeros_like(acc)
        l_ref[...] = jnp.zeros_like(l_ref)
        qn = jnp.max(qn_ref[...])
    else:
        acc[...] = acc_in[...]
        l_ref[...] = l_in[...]
        m_ref[...] = m_in[...]
        qn = jnp.max(m_in[nqb * pairs])

    base = 0
    for tok in toks:
        project(tok, wk, wvt, k_ref, vt_ref, norm_ref, base)
        base += tok.shape[0] // BLOCK
    fast = jnp.logical_and(qn < 1e20, qn * jnp.max(norm_ref[...]) <= 3600.0)
    if kind == FIRST:
        m_ref[...] = jnp.full_like(m_ref, jnp.where(fast, 0.0, LOW))
    m_ref[nqb * pairs] = jnp.full_like(m_ref[nqb * pairs], jnp.where(fast, qn, -LOW))
    count = plan[7, kind]

    def blocks(item):
        return jnp.maximum(plan[kind, 2 * item], 0), jnp.maximum(plan[kind, 2 * item + 1], 0)

    def scores(item):
        b0, b1 = blocks(item)
        bias0 = jnp.where(plan[kind, 2 * item] < 0, LOW, 0.0).astype(jnp.float32)
        bias1 = jnp.where(plan[kind, 2 * item + 1] < 0, LOW, 0.0).astype(jnp.float32)
        qb = plan[4 + kind, item]
        made = []
        for hp in range(pairs):
            cut = slice(hp * BLOCK, (hp + 1) * BLOCK)
            k = jnp.concatenate([k_ref[b0, :, cut], k_ref[b1, :, cut]], axis=0)
            s = jnp.dot(k, qbd[qb, hp], preferred_element_type=jnp.float32)
            made.append((s[:BLOCK] + bias0, s[BLOCK:] + bias1))
        return made

    def values(item, hp):
        b0, b1 = blocks(item)
        cut = slice(hp * BLOCK, (hp + 1) * BLOCK)
        v = jnp.concatenate([vt_ref[b0, cut, :], vt_ref[b1, cut, :]], axis=1)
        return jnp.concatenate([v, jnp.ones((16, 2 * BLOCK), jnp.bfloat16)], axis=0)

    @pl.when(fast)
    def _():
        def weigh(item, slot):
            for hp, halves in enumerate(scores(item)):
                for i, s in enumerate(halves):
                    p_ref[slot, hp, i * BLOCK:(i + 1) * BLOCK, :] = jnp.exp(s).astype(jnp.bfloat16)

        def gather(item, slot):
            qb = plan[4 + kind, item]
            pvs = [
                jnp.dot(values(item, hp), p_ref[slot, hp], preferred_element_type=jnp.float32)
                for hp in range(pairs)
            ]
            for hp, pv in enumerate(pvs):
                row = qb * pairs + hp
                acc[row, :64, :] = acc[row, :64, :] + pv[:64, :BLOCK]
                acc[row, 64:, :] = acc[row, 64:, :] + pv[64:BLOCK, BLOCK:]
                l_ref[row] = l_ref[row] + pv[BLOCK:BLOCK + 1, :]

        p_ref[1] = jnp.zeros_like(p_ref[1])

        def two(t, carry):
            gather(jnp.maximum(2 * t - 1, 0), 1)
            weigh(2 * t, 0)
            gather(2 * t, 0)
            weigh(2 * t + 1, 1)
            return carry

        lax.fori_loop(0, count, two, 0)
        gather(jnp.maximum(2 * count - 1, 0), 1)

    @pl.when(jnp.logical_not(fast))
    def _():
        def one(item, carry):
            qb = plan[4 + kind, item]
            for hp, halves in enumerate(scores(item)):
                row = qb * pairs + hp
                s = jnp.concatenate(halves, axis=0)
                m_old = m_ref[row]
                m_new = jnp.maximum(m_old, jnp.max(s, axis=0, keepdims=True))
                p = jnp.exp(s - m_new).astype(jnp.bfloat16)
                alpha = jnp.exp(m_old - m_new)
                pv = jnp.dot(values(item, hp), p, preferred_element_type=jnp.float32)
                acc[row, :64, :] = acc[row, :64, :] * alpha[:, :BLOCK] + pv[:64, :BLOCK]
                acc[row, 64:, :] = acc[row, 64:, :] * alpha[:, BLOCK:] + pv[64:BLOCK, BLOCK:]
                l_ref[row] = l_ref[row] * alpha + pv[BLOCK:BLOCK + 1, :]
                m_ref[row] = m_new
            return carry

        lax.fori_loop(0, 2 * count, one, 0)

    if kind == LAST:
        @pl.loop(0, nqb)
        def _(qb):
            parts = []
            for hp in range(pairs):
                row = qb * pairs + hp
                inv = 1.0 / l_ref[row]
                parts.append(acc[row, :64, :] * inv[:, :BLOCK])
                parts.append(acc[row, 64:, :] * inv[:, BLOCK:])
            ctx = jnp.concatenate(parts, axis=0).T.astype(jnp.bfloat16)
            out[pl.ds(pl.multiple_of(qb * BLOCK, BLOCK), BLOCK), :] = cast_dot(ctx, wo[...], ((1,), (0,)))


def run_phase(kind, toks, wk, wvt, nbound, lists=None, wqt=None, state=None, wo=None):
    width = wk.shape[0]
    pairs = width // BLOCK
    nkb = sum(t.shape[0] for t in toks) // BLOCK
    vmem, smem = pl.BlockSpec(memory_space=pltpu.VMEM), pl.BlockSpec(memory_space=pltpu.SMEM)
    args, specs = list(toks) + [wk, wvt], [vmem] * (len(toks) + 2)
    if kind == FIRST:
        args += list(lists) + [wqt]
        specs += [smem] * 3 + [vmem]
        nqb = toks[0].shape[0] // BLOCK
    else:
        args += list(state)
        specs += [smem] + [vmem] * 4
        nqb = state[1].shape[0]
    if kind == LAST:
        args.append(wo)
        specs.append(vmem)
    sums = [(nqb * pairs, BLOCK, BLOCK), (nqb * pairs + 1, 1, 2 * BLOCK), (nqb * pairs, 1, 2 * BLOCK)]
    outs, out_specs, scratch = [], [], []
    if kind == LAST:
        outs.append(jax.ShapeDtypeStruct((nqb * BLOCK, width), jnp.bfloat16))
        out_specs.append(vmem)
        scratch += [pltpu.VMEM(s, jnp.float32) for s in sums]
    else:
        if kind == FIRST:
            outs += [
                jax.ShapeDtypeStruct((8, PLAN_LEN), jnp.int32),
                jax.ShapeDtypeStruct((nqb, pairs, BLOCK, 2 * BLOCK), jnp.bfloat16),
            ]
            out_specs += [smem, vmem]
        outs += [jax.ShapeDtypeStruct(s, jnp.float32) for s in sums]
        out_specs += [vmem] * 3
    scratch += [
        pltpu.VMEM((nkb, BLOCK, width), jnp.bfloat16),
        pltpu.VMEM((nkb, width, BLOCK), jnp.bfloat16),
        pltpu.VMEM((2, pairs, 2 * BLOCK, 2 * BLOCK), jnp.bfloat16),
        pltpu.VMEM((1, BLOCK), jnp.float32),
    ]
    if kind == FIRST:
        scratch.append(pltpu.VMEM((1, ROWS), jnp.float32))
    units = {FIRST: 18, MIDDLE: 34, LAST: 43}[kind]
    cost = pl.CostEstimate(
        flops=units * 8 * 2 * BLOCK ** 3 * 8 + nkb * BLOCK * width * width * 4,
        bytes_accessed=8 << 20,
        transcendentals=units * 8 * BLOCK * BLOCK,
    )
    return pl.pallas_call(
        functools.partial(phase, kind, len(toks), nbound),
        out_shape=outs,
        in_specs=specs,
        out_specs=out_specs,
        scratch_shapes=scratch,
        compiler_params=pltpu.CompilerParams(vmem_limit_bytes=40 << 20),
        cost_estimate=cost,
        name=("attend_own", "attend_middle", "attend_last")[kind],
    )(*args)


def send(value, pairs):
    return lax.ppermute(value, "curve", pairs)


def on_device(tokens, w_query, w_keyval, w_out, block_list, block_count, bnd_ids):
    tok_dev, width = tokens.shape
    nbound = bnd_ids.shape[0]
    size = lax.axis_size("curve")
    member = lax.axis_index("curve")
    everyone = range(size)

    owner = bnd_ids // tok_dev
    slots = jnp.arange(BCAP, dtype=jnp.int32)
    my_start = jnp.sum((owner < member).astype(jnp.int32))
    padded_ids = jnp.concatenate([bnd_ids, jnp.zeros((BCAP,), jnp.int32)])
    my_ids = lax.dynamic_slice_in_dim(padded_ids, my_start, BCAP) - member * tok_dev
    pick = (my_ids[:, None] == jnp.arange(tok_dev, dtype=jnp.int32)[None, :]).astype(jnp.bfloat16)
    rows = jnp.dot(pick, tokens, preferred_element_type=jnp.float32).astype(jnp.bfloat16)
    gathered = lax.all_gather(rows, "curve", axis=0, tiled=True)

    from_two_behind = send(tokens, [(i, i + 2) for i in everyone if i + 2 < size])
    from_two_ahead = send(tokens, [(i, i - 2) for i in everyone if i >= 2])
    mate = send(tokens, [(i, i ^ 1) for i in everyone])

    wk = w_keyval[:, :width]
    wvt = w_keyval[:, width:].T
    lists = (member.reshape(1).astype(jnp.int32), block_list, block_count)
    plan, qbd, *sums = run_phase(FIRST, [tokens], wk, wvt, nbound, lists=lists, wqt=w_query.T)

    after = jnp.minimum(plan[7, 0], 0)
    half = tok_dev // 2
    relay = jnp.where(member % 2 == after, from_two_ahead[:half], from_two_behind[:half])
    low = send(relay, [(i, i ^ 1) for i in everyone])
    hops = [(i, i + 2 - 4 * (i % 2)) for i in everyone]
    upper = lax.dynamic_slice_in_dim(mate, half + after, half)
    high = send(upper, [(a, b) for a, b in hops if 0 <= b < size])

    sums = run_phase(
        MIDDLE, [from_two_behind, from_two_ahead, mate], wk, wvt, nbound, state=[plan, qbd, *sums]
    )

    slot_range = jnp.arange(nbound, dtype=jnp.int32)
    owner_start = jnp.sum((owner[None, :] < owner[:, None]).astype(jnp.int32), axis=1)
    done = (sums[1][-1, 0, 0] < LOW).astype(jnp.int32)
    source = owner * BCAP + slot_range - owner_start + done
    choose = (source[:, None] == jnp.arange(size * BCAP, dtype=jnp.int32)[None, :]).astype(jnp.bfloat16)
    bound = jnp.dot(choose, gathered, preferred_element_type=jnp.float32).astype(jnp.bfloat16)
    far = jnp.concatenate([low, high], axis=0)
    (mixed,) = run_phase(LAST, [far, bound], wk, wvt, nbound, state=[plan, qbd, *sums], wo=w_out)
    return mixed


def solution(mesh):
    in_specs = (
        P(("geo", "curve"), None),
        P(),
        P(),
        P(),
        P(("geo", "curve"), None),
        P(("geo", "curve")),
        P("geo"),
    )
    out_specs = P(("geo", "curve"), None)
    return jax.shard_map(
        on_device, mesh=mesh, in_specs=in_specs, out_specs=out_specs, check_vma=False
    )
```

```python
import functools

import jax
import jax.numpy as jnp
from jax import lax
from jax.experimental import pallas as pl
from jax.experimental.pallas import tpu as pltpu
from jax.sharding import PartitionSpec as P

HEADS = 8
BLOCK = 128
NB = 12
BCAP = 128
LOW = -1e30
ROWS = 256

FIRST, MIDDLE, LAST = range(3)
PLAN_LEN = 128


def cast_dot(a, b, dims):
    out = lax.dot_general(a, b, (dims, ((), ())), preferred_element_type=jnp.float32)
    return out.astype(jnp.bfloat16)


def project(tok, wk, wvt, k_ref, vt_ref, norm_ref, base):
    width = wvt.shape[0]
    feature = lax.broadcasted_iota(jnp.int32, (width, BLOCK), 0)
    head = lax.broadcasted_iota(jnp.int32, (width, BLOCK), 1)
    ind = jnp.where(feature >> 6 == head, 1.0, 0.0).astype(jnp.bfloat16)

    @pl.loop(0, tok.shape[0] // ROWS)
    def _(t):
        rows = tok[pl.ds(pl.multiple_of(t * ROWS, ROWS), ROWS), :]
        k = cast_dot(rows, wk[:, :width], ((1,), (0,)))
        vt = cast_dot(wvt[...], rows, ((1,), (1,)))
        for i in range(ROWS // BLOCK):
            at = base + t * (ROWS // BLOCK) + i
            k_ref[at] = k[i * BLOCK:(i + 1) * BLOCK, :]
            vt_ref[at] = vt[:, i * BLOCK:(i + 1) * BLOCK]
        norm = jnp.dot(k * k, ind, preferred_element_type=jnp.float32)
        norm_ref[...] = jnp.maximum(norm_ref[...], jnp.max(norm, axis=0, keepdims=True))


def plan_row(me, nqb, nbound, lists, counts, plan, qb, tops):
    used = counts[qb]
    near = 3 - 2 * lax.rem(me, 2)
    ns = list(tops)
    for i in range(NB):
        rel = jnp.clip(lists[qb, i] - (me - 2) * nqb, 0, 5 * nqb - 1)
        slot = lax.div(rel, nqb)
        src = jnp.where(slot == 4, 1, jnp.where(slot == near, 2, 0))
        block = src * nqb + rel - slot * nqb
        last = slot == 4 - near
        own = slot == 2
        live = (i < used).astype(jnp.int32)
        kind = jnp.where(own, FIRST, jnp.where(last, LAST, MIDDLE))
        for k in (FIRST, MIDDLE, LAST):
            plan[k, ns[k]] = block
            ns[k] = ns[k] + jnp.where(kind == k, live, 0)
    for k in (FIRST, MIDDLE, LAST):
        plan[k, ns[k]] = -1
        top = tops[k] + 2 * lax.div(ns[k] - tops[k] + 1, 2)
        if k == LAST:
            for j in range(nbound // BLOCK):
                plan[k, top + j] = nqb + j
            top = top + nbound // BLOCK
        first = lax.div(tops[k], 2)
        for j in range((NB + nbound // BLOCK) // 2 if k == LAST else NB // 2):
            plan[4 + k, first + j] = qb
        ns[k] = top
    return tuple(ns)


def plan_end(plan, tops):
    for k in (FIRST, MIDDLE, LAST):
        plan[k, tops[k]] = -1
        plan[k, tops[k] + 1] = -1
        plan[4 + k, lax.div(tops[k], 2)] = 0
        plan[7, k] = lax.div(tops[k] + 2, 4)


def pick_rows(me_ref, ids, tokens, out):
    me, tok_dev = me_ref[0], tokens.shape[0]
    n = ids.shape[1]
    mine = ids[...]
    start = jnp.sum(jnp.where(mine < me * tok_dev, 1.0, 0.0), axis=1, keepdims=True).astype(jnp.int32)
    r = lax.broadcasted_iota(jnp.int32, (BCAP, n), 0)
    j = lax.broadcasted_iota(jnp.int32, (BCAP, n), 1)
    local = (mine - me * tok_dev).astype(jnp.float32)
    spot = jnp.sum(jnp.where(j - r == start, local, 0.0), axis=1, keepdims=True).astype(jnp.int32)
    t = lax.broadcasted_iota(jnp.int32, (BCAP, tok_dev), 1)
    chosen = jnp.where(t == spot, 1.0, 0.0).astype(jnp.bfloat16)
    out[...] = cast_dot(chosen, tokens[...], ((1,), (0,)))


def join_rows(ids, gathered, out, tok_dev):
    n = ids.shape[1]
    size = gathered.shape[0] // BCAP
    mine = ids[...]
    j = lax.broadcasted_iota(jnp.int32, (n, BCAP), 0)
    r = lax.broadcasted_iota(jnp.int32, (n, BCAP), 1)
    starts = [
        jnp.sum(jnp.where(mine < o * tok_dev, 1.0, 0.0), axis=1, keepdims=True).astype(jnp.int32)
        for o in range(size + 1)
    ]
    parts = []
    for o in range(size):
        hit = jnp.logical_and(j - r == starts[o], r < starts[o + 1] - starts[o])
        parts.append(jnp.where(hit, 1.0, 0.0).astype(jnp.bfloat16))
    out[...] = cast_dot(jnp.concatenate(parts, axis=1), gathered[...], ((1,), (0,)))


def phase(kind, nsrc, nbound, *refs):
    refs = list(refs)
    take = lambda n: [refs.pop(0) for _ in range(n)]
    toks = take(nsrc)
    (wk,) = take(1)
    if kind == FIRST:
        me_ref, lists, counts, wq = take(4)
    else:
        wvt, plan, qbd, acc_in, m_in, l_in = take(6)
    if kind == LAST:
        ids, gathered, wo, out = take(4)
    elif kind == FIRST:
        wvt, plan, qbd = take(3)
    acc, m_ref, l_ref, k_ref, vt_ref, p_ref, norm_ref = take(7)
    nqb, pairs = qbd.shape[0], qbd.shape[1]

    norm_ref[...] = jnp.zeros_like(norm_ref)
    if kind == FIRST:
        qn_ref, wqt = take(2)
        wqt[...] = wq[...].T
        wvt[...] = wk[:, wvt.shape[0]:].T
        qn_ref[...] = jnp.zeros_like(qn_ref)
        zero = jnp.zeros((64, BLOCK), jnp.bfloat16)

        def query(t, tops):
            rows = toks[0][pl.ds(pl.multiple_of(t * ROWS, ROWS), ROWS), :]
            q = lax.dot_general(wqt[...], rows, (((1,), (1,)), ((), ())), preferred_element_type=jnp.float32)
            q = q.astype(jnp.bfloat16) * jnp.bfloat16(0.125)
            for i in range(ROWS // BLOCK):
                for hp in range(pairs):
                    cut = q[hp * BLOCK:(hp + 1) * BLOCK, i * BLOCK:(i + 1) * BLOCK]
                    at = t * (ROWS // BLOCK) + i
                    qbd[at, hp, :64, :] = jnp.concatenate([cut[:64], zero], axis=1)
                    qbd[at, hp, 64:, :] = jnp.concatenate([zero, cut[64:]], axis=1)
            q = q.astype(jnp.float32)
            for h in range(2 * pairs):
                part = q[h * 64:(h + 1) * 64, :]
                qn_ref[...] = jnp.maximum(qn_ref[...], jnp.sum(part * part, axis=0, keepdims=True))
            for i in range(ROWS // BLOCK):
                qb = t * (ROWS // BLOCK) + i
                tops = plan_row(me_ref[0], nqb, nbound, lists, counts, plan, qb, tops)
            return tops

        tops = lax.fori_loop(0, toks[0].shape[0] // ROWS, query, (jnp.int32(0),) * 3)
        plan_end(plan, tops)
        acc[...] = jnp.zeros_like(acc)
        l_ref[...] = jnp.zeros_like(l_ref)
        qn = jnp.max(qn_ref[...])
    else:
        acc[...] = acc_in[...]
        l_ref[...] = l_in[...]
        m_ref[...] = m_in[...]
        qn = jnp.max(m_in[nqb * pairs])

    base = 0
    if kind == LAST:
        (bound,) = take(1)
        join_rows(ids, gathered, bound, toks[0].shape[0])
        toks = toks + [bound]
    for tok in toks:
        project(tok, wk, wvt, k_ref, vt_ref, norm_ref, base)
        base += tok.shape[0] // BLOCK
    fast = jnp.logical_and(qn < 1e20, qn * jnp.max(norm_ref[...]) <= 3600.0)
    if kind == FIRST:
        m_ref[...] = jnp.full_like(m_ref, jnp.where(fast, 0.0, LOW))
    m_ref[nqb * pairs] = jnp.full_like(m_ref[nqb * pairs], jnp.where(fast, qn, -LOW))
    count = plan[7, kind]

    def blocks(item):
        return jnp.maximum(plan[kind, 2 * item], 0), jnp.maximum(plan[kind, 2 * item + 1], 0)

    def scores(item):
        b0, b1 = blocks(item)
        qb = plan[4 + kind, item]
        made = []
        for hp in range(pairs):
            cut = slice(hp * BLOCK, (hp + 1) * BLOCK)
            k = jnp.concatenate([k_ref[b0, :, cut], k_ref[b1, :, cut]], axis=0)
            made.append(jnp.dot(k, qbd[qb, hp], preferred_element_type=jnp.float32))
        return made

    def values(item, hp):
        b0, b1 = blocks(item)
        cut = slice(hp * BLOCK, (hp + 1) * BLOCK)
        halves = []
        for b, live in ((b0, plan[kind, 2 * item] >= 0), (b1, plan[kind, 2 * item + 1] >= 0)):
            v = jnp.concatenate([vt_ref[b, cut, :], jnp.ones((16, BLOCK), jnp.bfloat16)], axis=0)
            halves.append(v * jnp.where(live, 1.0, 0.0).astype(jnp.bfloat16))
        return jnp.concatenate(halves, axis=1)

    @pl.when(fast)
    def _():
        def weigh(item, slot):
            for hp, s in enumerate(scores(item)):
                p_ref[slot, hp] = jnp.exp(s).astype(jnp.bfloat16)

        def gather(item, slot):
            qb = plan[4 + kind, item]
            pvs = [
                jnp.dot(values(item, hp), p_ref[slot, hp], preferred_element_type=jnp.float32)
                for hp in range(pairs)
            ]
            for hp, pv in enumerate(pvs):
                row = qb * pairs + hp
                acc[row, :64, :] = acc[row, :64, :] + pv[:64, :BLOCK]
                acc[row, 64:, :] = acc[row, 64:, :] + pv[64:BLOCK, BLOCK:]
                l_ref[row] = l_ref[row] + pv[BLOCK:BLOCK + 1, :]

        p_ref[1] = jnp.zeros_like(p_ref[1])

        def two(t, carry):
            gather(jnp.maximum(2 * t - 1, 0), 1)
            weigh(2 * t, 0)
            gather(2 * t, 0)
            weigh(2 * t + 1, 1)
            return carry

        lax.fori_loop(0, count, two, 0)
        gather(jnp.maximum(2 * count - 1, 0), 1)

    @pl.when(jnp.logical_not(fast))
    def _():
        def one(item, carry):
            qb = plan[4 + kind, item]
            bias0 = jnp.where(plan[kind, 2 * item] < 0, LOW, 0.0).astype(jnp.float32)
            bias1 = jnp.where(plan[kind, 2 * item + 1] < 0, LOW, 0.0).astype(jnp.float32)
            for hp, s in enumerate(scores(item)):
                row = qb * pairs + hp
                s = jnp.concatenate([s[:BLOCK] + bias0, s[BLOCK:] + bias1], axis=0)
                m_old = m_ref[row]
                m_new = jnp.maximum(m_old, jnp.max(s, axis=0, keepdims=True))
                p = jnp.exp(s - m_new).astype(jnp.bfloat16)
                alpha = jnp.exp(m_old - m_new)
                pv = jnp.dot(values(item, hp), p, preferred_element_type=jnp.float32)
                acc[row, :64, :] = acc[row, :64, :] * alpha[:, :BLOCK] + pv[:64, :BLOCK]
                acc[row, 64:, :] = acc[row, 64:, :] * alpha[:, BLOCK:] + pv[64:BLOCK, BLOCK:]
                l_ref[row] = l_ref[row] * alpha + pv[BLOCK:BLOCK + 1, :]
                m_ref[row] = m_new
            return carry

        lax.fori_loop(0, 2 * count, one, 0)

    if kind == LAST:
        @pl.loop(0, nqb)
        def _(qb):
            parts = []
            for hp in range(pairs):
                row = qb * pairs + hp
                inv = 1.0 / l_ref[row]
                parts.append(acc[row, :64, :] * inv[:, :BLOCK])
                parts.append(acc[row, 64:, :] * inv[:, BLOCK:])
            ctx = jnp.concatenate(parts, axis=0).T.astype(jnp.bfloat16)
            out[pl.ds(pl.multiple_of(qb * BLOCK, BLOCK), BLOCK), :] = cast_dot(ctx, wo[...], ((1,), (0,)))


def run_phase(kind, toks, wk, nbound, lists=None, wq=None, state=None, ends=None):
    width = wk.shape[0]
    pairs = width // BLOCK
    nkb = sum(t.shape[0] for t in toks) // BLOCK + (nbound // BLOCK if kind == LAST else 0)
    vmem, smem = pl.BlockSpec(memory_space=pltpu.VMEM), pl.BlockSpec(memory_space=pltpu.SMEM)
    args, specs = list(toks) + [wk], [vmem] * (len(toks) + 1)
    if kind == FIRST:
        args += list(lists) + [wq]
        specs += [smem] * 3 + [vmem]
        nqb = toks[0].shape[0] // BLOCK
    else:
        args += list(state)
        specs += [vmem, smem] + [vmem] * 4
        nqb = state[2].shape[0]
    if kind == LAST:
        args += list(ends)
        specs += [vmem] * 3
    sums = [(nqb * pairs, BLOCK, BLOCK), (nqb * pairs + 1, 1, 2 * BLOCK), (nqb * pairs, 1, 2 * BLOCK)]
    outs, out_specs, scratch = [], [], []
    if kind == LAST:
        outs.append(jax.ShapeDtypeStruct((nqb * BLOCK, width), jnp.bfloat16))
        out_specs.append(vmem)
        scratch += [pltpu.VMEM(s, jnp.float32) for s in sums]
    else:
        if kind == FIRST:
            outs += [
                jax.ShapeDtypeStruct((width, width), jnp.bfloat16),
                jax.ShapeDtypeStruct((8, PLAN_LEN), jnp.int32),
                jax.ShapeDtypeStruct((nqb, pairs, BLOCK, 2 * BLOCK), jnp.bfloat16),
            ]
            out_specs += [vmem, smem, vmem]
        outs += [jax.ShapeDtypeStruct(s, jnp.float32) for s in sums]
        out_specs += [vmem] * 3
    scratch += [
        pltpu.VMEM((nkb, BLOCK, width), jnp.bfloat16),
        pltpu.VMEM((nkb, width, BLOCK), jnp.bfloat16),
        pltpu.VMEM((2, pairs, 2 * BLOCK, 2 * BLOCK), jnp.bfloat16),
        pltpu.VMEM((1, BLOCK), jnp.float32),
    ]
    if kind == FIRST:
        scratch += [pltpu.VMEM((1, ROWS), jnp.float32), pltpu.VMEM((width, width), jnp.bfloat16)]
    if kind == LAST:
        scratch.append(pltpu.VMEM((nbound, width), jnp.bfloat16))
    units = {FIRST: 18, MIDDLE: 34, LAST: 43}[kind]
    cost = pl.CostEstimate(
        flops=units * 8 * 2 * BLOCK ** 3 * 8 + nkb * BLOCK * width * width * 4,
        bytes_accessed=8 << 20,
        transcendentals=units * 8 * BLOCK * BLOCK,
    )
    return pl.pallas_call(
        functools.partial(phase, kind, len(toks), nbound),
        out_shape=outs,
        in_specs=specs,
        out_specs=out_specs,
        scratch_shapes=scratch,
        compiler_params=pltpu.CompilerParams(vmem_limit_bytes=24 << 20),
        cost_estimate=cost,
        name=("attend_own", "attend_middle", "attend_last")[kind],
    )(*args)


def send(value, pairs):
    return lax.ppermute(value, "curve", pairs)


def on_device(tokens, w_query, w_keyval, w_out, block_list, block_count, bnd_ids):
    tok_dev, width = tokens.shape
    nbound = bnd_ids.shape[0]
    size = lax.axis_size("curve")
    member = lax.axis_index("curve")
    everyone = range(size)

    vmem, smem = pl.BlockSpec(memory_space=pltpu.VMEM), pl.BlockSpec(memory_space=pltpu.SMEM)
    me = member.reshape(1).astype(jnp.int32)
    ids = bnd_ids.reshape(1, nbound)
    rows = pl.pallas_call(
        pick_rows,
        out_shape=jax.ShapeDtypeStruct((BCAP, width), jnp.bfloat16),
        in_specs=[smem, vmem, vmem],
        out_specs=vmem,
        compiler_params=pltpu.CompilerParams(vmem_limit_bytes=24 << 20),
        name="pick_rows",
    )(me, ids, tokens)
    gathered = lax.all_gather(rows, "curve", axis=0, tiled=True)

    from_two_behind = send(tokens, [(i, i + 2) for i in everyone if i + 2 < size])
    from_two_ahead = send(tokens, [(i, i - 2) for i in everyone if i >= 2])
    mate = send(tokens, [(i, i ^ 1) for i in everyone])

    wvt, plan, qbd, *sums = run_phase(
        FIRST, [tokens], w_keyval, nbound, lists=(me, block_list, block_count), wq=w_query
    )

    after = jnp.minimum(plan[7, 0], 0)
    half = tok_dev // 2
    relay = jnp.where(member % 2 == after, from_two_ahead[:half], from_two_behind[:half])
    low = send(relay, [(i, i ^ 1) for i in everyone])
    hops = [(i, i + 2 - 4 * (i % 2)) for i in everyone]
    upper = lax.dynamic_slice_in_dim(mate, half + after, half)
    high = send(upper, [(a, b) for a, b in hops if 0 <= b < size])

    sums = run_phase(
        MIDDLE,
        [from_two_behind, from_two_ahead, mate],
        w_keyval,
        nbound,
        state=[wvt, plan, qbd, *sums],
    )
    far = jnp.concatenate([low, high], axis=0)
    (mixed,) = run_phase(
        LAST, [far], w_keyval, nbound, state=[wvt, plan, qbd, *sums], ends=(ids, gathered, w_out)
    )
    return mixed


def solution(mesh):
    in_specs = (
        P(("geo", "curve"), None),
        P(),
        P(),
        P(),
        P(("geo", "curve"), None),
        P(("geo", "curve")),
        P("geo"),
    )
    out_specs = P(("geo", "curve"), None)
    return jax.shard_map(
        on_device, mesh=mesh, in_specs=in_specs, out_specs=out_specs, check_vma=False
    )
```

```python
import functools

import jax
import jax.numpy as jnp
from jax import lax
from jax.experimental import pallas as pl
from jax.experimental.pallas import tpu as pltpu
from jax.sharding import PartitionSpec as P

HEADS = 8
BLOCK = 128
NB = 12
BCAP = 128
LOW = -1e30
ROWS = 256

FIRST, MIDDLE, LAST = range(3)
PLAN_LEN = 128


def cast_dot(a, b, dims):
    out = lax.dot_general(a, b, (dims, ((), ())), preferred_element_type=jnp.float32)
    return out.astype(jnp.bfloat16)


def project(tok, wk, wvt, k_ref, vt_ref, norm_ref, base):
    width = wvt.shape[0]
    feature = lax.broadcasted_iota(jnp.int32, (width, BLOCK), 0)
    head = lax.broadcasted_iota(jnp.int32, (width, BLOCK), 1)
    ind = jnp.where(feature >> 6 == head, 1.0, 0.0).astype(jnp.bfloat16)

    @pl.loop(0, tok.shape[0] // ROWS)
    def _(t):
        rows = tok[pl.ds(pl.multiple_of(t * ROWS, ROWS), ROWS), :]
        k = cast_dot(rows, wk[:, :width], ((1,), (0,)))
        vt = cast_dot(wvt[...], rows, ((1,), (1,)))
        for i in range(ROWS // BLOCK):
            at = base + t * (ROWS // BLOCK) + i
            k_ref[at] = k[i * BLOCK:(i + 1) * BLOCK, :]
            vt_ref[at] = vt[:, i * BLOCK:(i + 1) * BLOCK]
        norm = jnp.dot(k * k, ind, preferred_element_type=jnp.float32)
        norm_ref[...] = jnp.maximum(norm_ref[...], jnp.max(norm, axis=0, keepdims=True))


def plan_row(me, nqb, nbound, lists, counts, plan, qb, tops):
    used = counts[qb]
    near = 3 - 2 * lax.rem(me, 2)
    ns = list(tops)
    for i in range(NB):
        rel = jnp.clip(lists[qb, i] - (me - 2) * nqb, 0, 5 * nqb - 1)
        slot = lax.div(rel, nqb)
        src = jnp.where(slot == 4, 1, jnp.where(slot == near, 2, 0))
        block = src * nqb + rel - slot * nqb
        last = slot == 4 - near
        own = slot == 2
        live = (i < used).astype(jnp.int32)
        kind = jnp.where(own, FIRST, jnp.where(last, LAST, MIDDLE))
        for k in (FIRST, MIDDLE, LAST):
            plan[k, ns[k]] = block
            ns[k] = ns[k] + jnp.where(kind == k, live, 0)
    for k in (FIRST, MIDDLE, LAST):
        plan[k, ns[k]] = -1
        top = tops[k] + 2 * lax.div(ns[k] - tops[k] + 1, 2)
        if k == LAST:
            for j in range(nbound // BLOCK):
                plan[k, top + j] = nqb + j
            top = top + nbound // BLOCK
        first = lax.div(tops[k], 2)
        for j in range((NB + nbound // BLOCK) // 2 if k == LAST else NB // 2):
            plan[4 + k, first + j] = qb
        ns[k] = top
    return tuple(ns)


def plan_end(plan, tops):
    for k in (FIRST, MIDDLE, LAST):
        plan[k, tops[k]] = -1
        plan[k, tops[k] + 1] = -1
        plan[4 + k, lax.div(tops[k], 2)] = 0
        plan[7, k] = lax.div(tops[k] + 2, 4)


def pick_rows(me_ref, ids, tokens, out):
    me, tok_dev = me_ref[0], tokens.shape[0]
    n = ids.shape[1]
    mine = ids[...]
    start = jnp.sum(jnp.where(mine < me * tok_dev, 1.0, 0.0), axis=1, keepdims=True).astype(jnp.int32)
    r = lax.broadcasted_iota(jnp.int32, (BCAP, n), 0)
    j = lax.broadcasted_iota(jnp.int32, (BCAP, n), 1)
    local = (mine - me * tok_dev).astype(jnp.float32)
    spot = jnp.sum(jnp.where(j - r == start, local, 0.0), axis=1, keepdims=True).astype(jnp.int32)
    t = lax.broadcasted_iota(jnp.int32, (BCAP, tok_dev), 1)
    chosen = jnp.where(t == spot, 1.0, 0.0).astype(jnp.bfloat16)
    out[...] = cast_dot(chosen, tokens[...], ((1,), (0,)))


def join_rows(ids, gathered, out, tok_dev):
    n = ids.shape[1]
    size = gathered.shape[0] // BCAP
    mine = ids[...]
    j = lax.broadcasted_iota(jnp.int32, (n, BCAP), 0)
    r = lax.broadcasted_iota(jnp.int32, (n, BCAP), 1)
    starts = [
        jnp.sum(jnp.where(mine < o * tok_dev, 1.0, 0.0), axis=1, keepdims=True).astype(jnp.int32)
        for o in range(size + 1)
    ]
    parts = []
    for o in range(size):
        hit = jnp.logical_and(j - r == starts[o], r < starts[o + 1] - starts[o])
        parts.append(jnp.where(hit, 1.0, 0.0).astype(jnp.bfloat16))
    out[...] = cast_dot(jnp.concatenate(parts, axis=1), gathered[...], ((1,), (0,)))


def phase(kind, nsrc, nbound, *refs):
    refs = list(refs)
    take = lambda n: [refs.pop(0) for _ in range(n)]
    nin = nsrc + {FIRST: 2, MIDDLE: 6, LAST: 8}[kind]
    hbm_in = take(nin)
    if kind == FIRST:
        me_ref, lists, counts = take(3)
    else:
        (plan,) = take(1)
    if kind == LAST:
        ids, out = take(2)
    else:
        if kind == FIRST:
            wvt_out, plan, qbd_out = take(3)
        acc_out, m_out, l_out = take(3)
    bufs = take(nin)
    loads = []
    in_sem, out_sem = refs[-2:]
    for i in range(nin):
        loads.append(pltpu.make_async_copy(hbm_in[i], bufs[i], in_sem.at[i]))
        loads[i].start()
    wk, toks = bufs[0], bufs[2:2 + nsrc]
    if kind == FIRST:
        wq = bufs[1]
        wvt, qbd, acc, m_ref, l_ref = take(5)
    else:
        wvt, qbd = bufs[1], bufs[2 + nsrc]
        acc, m_ref, l_ref = bufs[3 + nsrc:6 + nsrc]
        if kind == LAST:
            gathered, wo = bufs[6 + nsrc:8 + nsrc]
    k_ref, vt_ref, p_ref, norm_ref = take(4)
    nqb, pairs = qbd.shape[0], qbd.shape[1]

    norm_ref[...] = jnp.zeros_like(norm_ref)
    if kind == FIRST:
        qn_ref, wqt = take(2)
        for load in loads:
            load.wait()
        wqt[...] = wq[...].T
        wvt[...] = wk[:, wvt.shape[0]:].T
        qn_ref[...] = jnp.zeros_like(qn_ref)
        zero = jnp.zeros((64, BLOCK), jnp.bfloat16)

        def query(t, tops):
            rows = toks[0][pl.ds(pl.multiple_of(t * ROWS, ROWS), ROWS), :]
            q = lax.dot_general(wqt[...], rows, (((1,), (1,)), ((), ())), preferred_element_type=jnp.float32)
            q = q.astype(jnp.bfloat16) * jnp.bfloat16(0.125)
            for i in range(ROWS // BLOCK):
                for hp in range(pairs):
                    cut = q[hp * BLOCK:(hp + 1) * BLOCK, i * BLOCK:(i + 1) * BLOCK]
                    at = t * (ROWS // BLOCK) + i
                    qbd[at, hp, :64, :] = jnp.concatenate([cut[:64], zero], axis=1)
                    qbd[at, hp, 64:, :] = jnp.concatenate([zero, cut[64:]], axis=1)
            q = q.astype(jnp.float32)
            for h in range(2 * pairs):
                part = q[h * 64:(h + 1) * 64, :]
                qn_ref[...] = jnp.maximum(qn_ref[...], jnp.sum(part * part, axis=0, keepdims=True))
            for i in range(ROWS // BLOCK):
                qb = t * (ROWS // BLOCK) + i
                tops = plan_row(me_ref[0], nqb, nbound, lists, counts, plan, qb, tops)
            return tops

        tops = lax.fori_loop(0, toks[0].shape[0] // ROWS, query, (jnp.int32(0),) * 3)
        plan_end(plan, tops)
        acc[...] = jnp.zeros_like(acc)
        l_ref[...] = jnp.zeros_like(l_ref)
        qn = jnp.max(qn_ref[...])
    else:
        loads[0].wait()
        loads[1].wait()

    base = 0
    for i, tok in enumerate(toks):
        if kind != FIRST:
            loads[2 + i].wait()
        project(tok, wk, wvt, k_ref, vt_ref, norm_ref, base)
        base += tok.shape[0] // BLOCK
    if kind != FIRST:
        for load in loads[2 + nsrc:]:
            load.wait()
        qn = jnp.max(m_ref[nqb * pairs])
    if kind == LAST:
        (bound,) = take(1)
        join_rows(ids, gathered, bound, toks[0].shape[0])
        project(bound, wk, wvt, k_ref, vt_ref, norm_ref, base)
    fast = jnp.logical_and(qn < 1e20, qn * jnp.max(norm_ref[...]) <= 3600.0)
    if kind == FIRST:
        m_ref[...] = jnp.full_like(m_ref, jnp.where(fast, 0.0, LOW))
    m_ref[nqb * pairs] = jnp.full_like(m_ref[nqb * pairs], jnp.where(fast, qn, -LOW))
    count = plan[7, kind]

    def blocks(item):
        return jnp.maximum(plan[kind, 2 * item], 0), jnp.maximum(plan[kind, 2 * item + 1], 0)

    def scores(item):
        b0, b1 = blocks(item)
        qb = plan[4 + kind, item]
        made = []
        for hp in range(pairs):
            cut = slice(hp * BLOCK, (hp + 1) * BLOCK)
            k = jnp.concatenate([k_ref[b0, :, cut], k_ref[b1, :, cut]], axis=0)
            made.append(jnp.dot(k, qbd[qb, hp], preferred_element_type=jnp.float32))
        return made

    def values(item, hp):
        b0, b1 = blocks(item)
        cut = slice(hp * BLOCK, (hp + 1) * BLOCK)
        halves = []
        for b, live in ((b0, plan[kind, 2 * item] >= 0), (b1, plan[kind, 2 * item + 1] >= 0)):
            v = jnp.concatenate([vt_ref[b, cut, :], jnp.ones((16, BLOCK), jnp.bfloat16)], axis=0)
            halves.append(v * jnp.where(live, 1.0, 0.0).astype(jnp.bfloat16))
        return jnp.concatenate(halves, axis=1)

    @pl.when(fast)
    def _():
        def weigh(item, slot):
            for hp, s in enumerate(scores(item)):
                p_ref[slot, hp] = jnp.exp(s).astype(jnp.bfloat16)

        def gather(item, slot):
            qb = plan[4 + kind, item]
            pvs = [
                jnp.dot(values(item, hp), p_ref[slot, hp], preferred_element_type=jnp.float32)
                for hp in range(pairs)
            ]
            for hp, pv in enumerate(pvs):
                row = qb * pairs + hp
                acc[row, :64, :] = acc[row, :64, :] + pv[:64, :BLOCK]
                acc[row, 64:, :] = acc[row, 64:, :] + pv[64:BLOCK, BLOCK:]
                l_ref[row] = l_ref[row] + pv[BLOCK:BLOCK + 1, :]

        p_ref[1] = jnp.zeros_like(p_ref[1])

        def two(t, carry):
            gather(jnp.maximum(2 * t - 1, 0), 1)
            weigh(2 * t, 0)
            gather(2 * t, 0)
            weigh(2 * t + 1, 1)
            return carry

        lax.fori_loop(0, count, two, 0)
        gather(jnp.maximum(2 * count - 1, 0), 1)

    @pl.when(jnp.logical_not(fast))
    def _():
        def one(item, carry):
            qb = plan[4 + kind, item]
            bias0 = jnp.where(plan[kind, 2 * item] < 0, LOW, 0.0).astype(jnp.float32)
            bias1 = jnp.where(plan[kind, 2 * item + 1] < 0, LOW, 0.0).astype(jnp.float32)
            for hp, s in enumerate(scores(item)):
                row = qb * pairs + hp
                s = jnp.concatenate([s[:BLOCK] + bias0, s[BLOCK:] + bias1], axis=0)
                m_old = m_ref[row]
                m_new = jnp.maximum(m_old, jnp.max(s, axis=0, keepdims=True))
                p = jnp.exp(s - m_new).astype(jnp.bfloat16)
                alpha = jnp.exp(m_old - m_new)
                pv = jnp.dot(values(item, hp), p, preferred_element_type=jnp.float32)
                acc[row, :64, :] = acc[row, :64, :] * alpha[:, :BLOCK] + pv[:64, :BLOCK]
                acc[row, 64:, :] = acc[row, 64:, :] * alpha[:, BLOCK:] + pv[64:BLOCK, BLOCK:]
                l_ref[row] = l_ref[row] * alpha + pv[BLOCK:BLOCK + 1, :]
                m_ref[row] = m_new
            return carry

        lax.fori_loop(0, 2 * count, one, 0)

    if kind != LAST:
        stores = [(acc, acc_out), (m_ref, m_out), (l_ref, l_out)]
        if kind == FIRST:
            stores += [(wvt, wvt_out), (qbd, qbd_out)]
        stores = [pltpu.make_async_copy(x, y, out_sem.at[i]) for i, (x, y) in enumerate(stores)]
        for store in stores:
            store.start()
        for store in stores:
            store.wait()

    if kind == LAST:
        @pl.loop(0, nqb)
        def _(qb):
            parts = []
            for hp in range(pairs):
                row = qb * pairs + hp
                inv = 1.0 / l_ref[row]
                parts.append(acc[row, :64, :] * inv[:, :BLOCK])
                parts.append(acc[row, 64:, :] * inv[:, BLOCK:])
            ctx = jnp.concatenate(parts, axis=0).T.astype(jnp.bfloat16)
            out[pl.ds(pl.multiple_of(qb * BLOCK, BLOCK), BLOCK), :] = cast_dot(ctx, wo[...], ((1,), (0,)))


def run_phase(kind, toks, wk, nbound, lists=None, wq=None, state=None, ends=None):
    width = wk.shape[0]
    pairs = width // BLOCK
    nkb = sum(t.shape[0] for t in toks) // BLOCK + (nbound // BLOCK if kind == LAST else 0)
    vmem, smem = pl.BlockSpec(memory_space=pltpu.VMEM), pl.BlockSpec(memory_space=pltpu.SMEM)
    hbm = pl.BlockSpec(memory_space=pltpu.HBM)
    if kind == FIRST:
        big, small = [wk, wq, *toks], list(lists)
        small_specs = [smem] * 3
        nqb = toks[0].shape[0] // BLOCK
    else:
        wvt, plan, qbd, *sums = state
        big, small = [wk, wvt, *toks, qbd, *sums], [plan]
        small_specs = [smem]
        nqb = qbd.shape[0]
    if kind == LAST:
        ids, gathered, wo = ends
        big += [gathered, wo]
        small.append(ids)
        small_specs.append(vmem)
    args, specs = big + small, [hbm] * len(big) + small_specs
    shapes = [(nqb * pairs, BLOCK, BLOCK), (nqb * pairs + 1, 1, 2 * BLOCK), (nqb * pairs, 1, 2 * BLOCK)]
    q_shape = (nqb, pairs, BLOCK, 2 * BLOCK)
    outs, out_specs = [], []
    scratch = [pltpu.VMEM(x.shape, x.dtype) for x in big]
    if kind == LAST:
        outs.append(jax.ShapeDtypeStruct((nqb * BLOCK, width), jnp.bfloat16))
        out_specs.append(vmem)
    else:
        if kind == FIRST:
            outs += [
                jax.ShapeDtypeStruct((width, width), jnp.bfloat16),
                jax.ShapeDtypeStruct((8, PLAN_LEN), jnp.int32),
                jax.ShapeDtypeStruct(q_shape, jnp.bfloat16),
            ]
            out_specs += [hbm, smem, hbm]
            scratch += [pltpu.VMEM((width, width), jnp.bfloat16), pltpu.VMEM(q_shape, jnp.bfloat16)]
            scratch += [pltpu.VMEM(s, jnp.float32) for s in shapes]
        outs += [jax.ShapeDtypeStruct(s, jnp.float32) for s in shapes]
        out_specs += [hbm] * 3
    scratch += [
        pltpu.VMEM((nkb, BLOCK, width), jnp.bfloat16),
        pltpu.VMEM((nkb, width, BLOCK), jnp.bfloat16),
        pltpu.VMEM((2, pairs, 2 * BLOCK, 2 * BLOCK), jnp.bfloat16),
        pltpu.VMEM((1, BLOCK), jnp.float32),
    ]
    if kind == FIRST:
        scratch += [pltpu.VMEM((1, ROWS), jnp.float32), pltpu.VMEM((width, width), jnp.bfloat16)]
    if kind == LAST:
        scratch.append(pltpu.VMEM((nbound, width), jnp.bfloat16))
    scratch += [pltpu.SemaphoreType.DMA((len(big),)), pltpu.SemaphoreType.DMA((5,))]
    units = {FIRST: 18, MIDDLE: 34, LAST: 43}[kind]
    cost = pl.CostEstimate(
        flops=units * 8 * 2 * BLOCK ** 3 * 8 + nkb * BLOCK * width * width * 4,
        bytes_accessed=8 << 20,
        transcendentals=units * 8 * BLOCK * BLOCK,
    )
    return pl.pallas_call(
        functools.partial(phase, kind, len(toks), nbound),
        out_shape=outs,
        in_specs=specs,
        out_specs=out_specs,
        scratch_shapes=scratch,
        compiler_params=pltpu.CompilerParams(vmem_limit_bytes=63 << 20),
        cost_estimate=cost,
        name=("attend_own", "attend_middle", "attend_last")[kind],
    )(*args)


def send(value, pairs):
    return lax.ppermute(value, "curve", pairs)


def on_device(tokens, w_query, w_keyval, w_out, block_list, block_count, bnd_ids):
    tok_dev, width = tokens.shape
    nbound = bnd_ids.shape[0]
    size = lax.axis_size("curve")
    member = lax.axis_index("curve")
    everyone = range(size)

    vmem, smem = pl.BlockSpec(memory_space=pltpu.VMEM), pl.BlockSpec(memory_space=pltpu.SMEM)
    me = member.reshape(1).astype(jnp.int32)
    ids = bnd_ids.reshape(1, nbound)
    rows = pl.pallas_call(
        pick_rows,
        out_shape=jax.ShapeDtypeStruct((BCAP, width), jnp.bfloat16),
        in_specs=[smem, vmem, vmem],
        out_specs=vmem,
        compiler_params=pltpu.CompilerParams(vmem_limit_bytes=63 << 20),
        name="pick_rows",
    )(me, ids, tokens)
    gathered = lax.all_gather(rows, "curve", axis=0, tiled=True)

    from_two_behind = send(tokens, [(i, i + 2) for i in everyone if i + 2 < size])
    from_two_ahead = send(tokens, [(i, i - 2) for i in everyone if i >= 2])
    mate = send(tokens, [(i, i ^ 1) for i in everyone])

    wvt, plan, qbd, *sums = run_phase(
        FIRST, [tokens], w_keyval, nbound, lists=(me, block_list, block_count), wq=w_query
    )

    after = jnp.minimum(plan[7, 0], 0)
    half = tok_dev // 2
    relay = jnp.where(member % 2 == after, from_two_ahead[:half], from_two_behind[:half])
    low = send(relay, [(i, i ^ 1) for i in everyone])
    hops = [(i, i + 2 - 4 * (i % 2)) for i in everyone]
    upper = lax.dynamic_slice_in_dim(mate, half + after, half)
    high = send(upper, [(a, b) for a, b in hops if 0 <= b < size])

    sums = run_phase(
        MIDDLE,
        [from_two_behind, from_two_ahead, mate],
        w_keyval,
        nbound,
        state=[wvt, plan, qbd, *sums],
    )
    far = jnp.concatenate([low, high], axis=0)
    (mixed,) = run_phase(
        LAST, [far], w_keyval, nbound, state=[wvt, plan, qbd, *sums], ends=(ids, gathered, w_out)
    )
    return mixed


def solution(mesh):
    in_specs = (
        P(("geo", "curve"), None),
        P(),
        P(),
        P(),
        P(("geo", "curve"), None),
        P(("geo", "curve")),
        P("geo"),
    )
    out_specs = P(("geo", "curve"), None)
    return jax.shard_map(
        on_device, mesh=mesh, in_specs=in_specs, out_specs=out_specs, check_vma=False
    )
```

```python
import functools

import jax
import jax.numpy as jnp
from jax import lax
from jax.experimental import pallas as pl
from jax.experimental.pallas import tpu as pltpu
from jax.sharding import PartitionSpec as P

HEADS = 8
BLOCK = 128
NB = 12
BCAP = 128
LOW = -1e30
ROWS = 256

FIRST, MIDDLE, LAST = range(3)
PLAN_LEN = 128


def cast_dot(a, b, dims):
    out = lax.dot_general(a, b, (dims, ((), ())), preferred_element_type=jnp.float32)
    return out.astype(jnp.bfloat16)


def project(tok, wk, wvt, k_ref, vt_ref, norm_ref, base):
    width = wvt.shape[0]
    feature = lax.broadcasted_iota(jnp.int32, (width, BLOCK), 0)
    head = lax.broadcasted_iota(jnp.int32, (width, BLOCK), 1)
    ind = jnp.where(feature >> 6 == head, 1.0, 0.0).astype(jnp.bfloat16)

    @pl.loop(0, tok.shape[0] // ROWS)
    def _(t):
        rows = tok[pl.ds(pl.multiple_of(t * ROWS, ROWS), ROWS), :]
        k = cast_dot(rows, wk[:, :width], ((1,), (0,)))
        vt = cast_dot(wvt[...], rows, ((1,), (1,)))
        for i in range(ROWS // BLOCK):
            at = base + t * (ROWS // BLOCK) + i
            k_ref[at] = k[i * BLOCK:(i + 1) * BLOCK, :]
            vt_ref[at] = vt[:, i * BLOCK:(i + 1) * BLOCK]
        norm = jnp.dot(k * k, ind, preferred_element_type=jnp.float32)
        norm_ref[...] = jnp.maximum(norm_ref[...], jnp.max(norm, axis=0, keepdims=True))


def plan_row(me, nqb, nbound, lists, counts, plan, qb, tops):
    used = counts[qb]
    near = 3 - 2 * lax.rem(me, 2)
    ns = list(tops)
    for i in range(NB):
        rel = jnp.clip(lists[qb, i] - (me - 2) * nqb, 0, 5 * nqb - 1)
        slot = lax.div(rel, nqb)
        src = jnp.where(slot == 4, 1, jnp.where(slot == near, 2, 0))
        block = src * nqb + rel - slot * nqb
        last = slot == 4 - near
        own = slot == 2
        live = (i < used).astype(jnp.int32)
        kind = jnp.where(own, FIRST, jnp.where(last, LAST, MIDDLE))
        for k in (FIRST, MIDDLE, LAST):
            plan[k, ns[k]] = block
            ns[k] = ns[k] + jnp.where(kind == k, live, 0)
    for k in (FIRST, MIDDLE, LAST):
        plan[k, ns[k]] = -1
        top = tops[k] + 2 * lax.div(ns[k] - tops[k] + 1, 2)
        if k == LAST:
            for j in range(nbound // BLOCK):
                plan[k, top + j] = nqb + j
            top = top + nbound // BLOCK
        first = lax.div(tops[k], 2)
        for j in range((NB + nbound // BLOCK) // 2 if k == LAST else NB // 2):
            plan[4 + k, first + j] = qb
        ns[k] = top
    return tuple(ns)


def plan_end(plan, tops):
    for k in (FIRST, MIDDLE, LAST):
        plan[k, tops[k]] = -1
        plan[k, tops[k] + 1] = -1
        plan[4 + k, lax.div(tops[k], 2)] = 0
        plan[7, k] = lax.div(tops[k] + 2, 4)


def pick_rows(me_ref, ids, tokens, out):
    me, tok_dev = me_ref[0], tokens.shape[0]
    n = ids.shape[1]
    mine = ids[...]
    start = jnp.sum(jnp.where(mine < me * tok_dev, 1.0, 0.0), axis=1, keepdims=True).astype(jnp.int32)
    r = lax.broadcasted_iota(jnp.int32, (BCAP, n), 0)
    j = lax.broadcasted_iota(jnp.int32, (BCAP, n), 1)
    local = (mine - me * tok_dev).astype(jnp.float32)
    spot = jnp.sum(jnp.where(j - r == start, local, 0.0), axis=1, keepdims=True).astype(jnp.int32)
    t = lax.broadcasted_iota(jnp.int32, (BCAP, tok_dev), 1)
    chosen = jnp.where(t == spot, 1.0, 0.0).astype(jnp.bfloat16)
    out[...] = cast_dot(chosen, tokens[...], ((1,), (0,)))


def join_rows(ids, gathered, out, tok_dev):
    n = ids.shape[1]
    size = gathered.shape[0] // BCAP
    mine = ids[...]
    j = lax.broadcasted_iota(jnp.int32, (n, BCAP), 0)
    r = lax.broadcasted_iota(jnp.int32, (n, BCAP), 1)
    starts = [
        jnp.sum(jnp.where(mine < o * tok_dev, 1.0, 0.0), axis=1, keepdims=True).astype(jnp.int32)
        for o in range(size + 1)
    ]
    parts = []
    for o in range(size):
        hit = jnp.logical_and(j - r == starts[o], r < starts[o + 1] - starts[o])
        parts.append(jnp.where(hit, 1.0, 0.0).astype(jnp.bfloat16))
    out[...] = cast_dot(jnp.concatenate(parts, axis=1), gathered[...], ((1,), (0,)))


def phase(kind, nsrc, nbound, *refs):
    refs = list(refs)
    take = lambda n: [refs.pop(0) for _ in range(n)]
    nin = nsrc + {FIRST: 2, MIDDLE: 6, LAST: 8}[kind]
    hbm_in = take(nin)
    if kind == FIRST:
        me_ref, lists, counts = take(3)
    else:
        (plan,) = take(1)
    if kind == LAST:
        ids, out = take(2)
    else:
        if kind == FIRST:
            wvt_out, plan, qbd_out, tok_out = take(4)
        acc_out, m_out, l_out = take(3)
    bufs = take(nin)
    loads = []
    in_sem, out_sem = refs[-2:]
    for i in range(nin):
        loads.append(pltpu.make_async_copy(hbm_in[i], bufs[i], in_sem.at[i]))
        loads[i].start()
    if kind == FIRST:
        again = pltpu.make_async_copy(hbm_in[2], tok_out, out_sem.at[5])
        again.start()
    wk, toks = bufs[0], bufs[2:2 + nsrc]
    if kind == FIRST:
        wq = bufs[1]
        wvt, qbd, acc, m_ref, l_ref = take(5)
    else:
        wvt, qbd = bufs[1], bufs[2 + nsrc]
        acc, m_ref, l_ref = bufs[3 + nsrc:6 + nsrc]
        if kind == LAST:
            gathered, wo = bufs[6 + nsrc:8 + nsrc]
    k_ref, vt_ref, p_ref, norm_ref = take(4)
    nqb, pairs = qbd.shape[0], qbd.shape[1]

    norm_ref[...] = jnp.zeros_like(norm_ref)
    if kind == FIRST:
        qn_ref, wqt = take(2)
        for load in loads:
            load.wait()
        wqt[...] = wq[...].T
        wvt[...] = wk[:, wvt.shape[0]:].T
        qn_ref[...] = jnp.zeros_like(qn_ref)
        zero = jnp.zeros((64, BLOCK), jnp.bfloat16)

        def query(t, tops):
            rows = toks[0][pl.ds(pl.multiple_of(t * ROWS, ROWS), ROWS), :]
            q = lax.dot_general(wqt[...], rows, (((1,), (1,)), ((), ())), preferred_element_type=jnp.float32)
            q = q.astype(jnp.bfloat16) * jnp.bfloat16(0.125)
            for i in range(ROWS // BLOCK):
                for hp in range(pairs):
                    cut = q[hp * BLOCK:(hp + 1) * BLOCK, i * BLOCK:(i + 1) * BLOCK]
                    at = t * (ROWS // BLOCK) + i
                    qbd[at, hp, :64, :] = jnp.concatenate([cut[:64], zero], axis=1)
                    qbd[at, hp, 64:, :] = jnp.concatenate([zero, cut[64:]], axis=1)
            q = q.astype(jnp.float32)
            for h in range(2 * pairs):
                part = q[h * 64:(h + 1) * 64, :]
                qn_ref[...] = jnp.maximum(qn_ref[...], jnp.sum(part * part, axis=0, keepdims=True))
            for i in range(ROWS // BLOCK):
                qb = t * (ROWS // BLOCK) + i
                tops = plan_row(me_ref[0], nqb, nbound, lists, counts, plan, qb, tops)
            return tops

        tops = lax.fori_loop(0, toks[0].shape[0] // ROWS, query, (jnp.int32(0),) * 3)
        plan_end(plan, tops)
        acc[...] = jnp.zeros_like(acc)
        l_ref[...] = jnp.zeros_like(l_ref)
        qn = jnp.max(qn_ref[...])
    else:
        loads[0].wait()
        loads[1].wait()

    base = 0
    for i, tok in enumerate(toks):
        if kind != FIRST:
            loads[2 + i].wait()
        project(tok, wk, wvt, k_ref, vt_ref, norm_ref, base)
        base += tok.shape[0] // BLOCK
    if kind != FIRST:
        for load in loads[2 + nsrc:]:
            load.wait()
        qn = jnp.max(m_ref[nqb * pairs])
    if kind == LAST:
        (bound,) = take(1)
        join_rows(ids, gathered, bound, toks[0].shape[0])
        project(bound, wk, wvt, k_ref, vt_ref, norm_ref, base)
    fast = jnp.logical_and(qn < 1e20, qn * jnp.max(norm_ref[...]) <= 3600.0)
    if kind == FIRST:
        m_ref[...] = jnp.full_like(m_ref, jnp.where(fast, 0.0, LOW))
    m_ref[nqb * pairs] = jnp.full_like(m_ref[nqb * pairs], jnp.where(fast, qn, -LOW))
    count = plan[7, kind]

    def blocks(item):
        return jnp.maximum(plan[kind, 2 * item], 0), jnp.maximum(plan[kind, 2 * item + 1], 0)

    def scores(item):
        b0, b1 = blocks(item)
        qb = plan[4 + kind, item]
        made = []
        for hp in range(pairs):
            cut = slice(hp * BLOCK, (hp + 1) * BLOCK)
            k = jnp.concatenate([k_ref[b0, :, cut], k_ref[b1, :, cut]], axis=0)
            made.append(jnp.dot(k, qbd[qb, hp], preferred_element_type=jnp.float32))
        return made

    def values(item, hp):
        b0, b1 = blocks(item)
        cut = slice(hp * BLOCK, (hp + 1) * BLOCK)
        halves = []
        for b, live in ((b0, plan[kind, 2 * item] >= 0), (b1, plan[kind, 2 * item + 1] >= 0)):
            v = jnp.concatenate([vt_ref[b, cut, :], jnp.ones((16, BLOCK), jnp.bfloat16)], axis=0)
            halves.append(v * jnp.where(live, 1.0, 0.0).astype(jnp.bfloat16))
        return jnp.concatenate(halves, axis=1)

    @pl.when(fast)
    def _():
        def weigh(item, slot):
            for hp, s in enumerate(scores(item)):
                p_ref[slot, hp] = jnp.exp(s).astype(jnp.bfloat16)

        def gather(item, slot):
            qb = plan[4 + kind, item]
            pvs = [
                jnp.dot(values(item, hp), p_ref[slot, hp], preferred_element_type=jnp.float32)
                for hp in range(pairs)
            ]
            for hp, pv in enumerate(pvs):
                row = qb * pairs + hp
                acc[row, :64, :] = acc[row, :64, :] + pv[:64, :BLOCK]
                acc[row, 64:, :] = acc[row, 64:, :] + pv[64:BLOCK, BLOCK:]
                l_ref[row] = l_ref[row] + pv[BLOCK:BLOCK + 1, :]

        p_ref[1] = jnp.zeros_like(p_ref[1])

        def two(t, carry):
            gather(jnp.maximum(2 * t - 1, 0), 1)
            weigh(2 * t, 0)
            gather(2 * t, 0)
            weigh(2 * t + 1, 1)
            return carry

        lax.fori_loop(0, count, two, 0)
        gather(jnp.maximum(2 * count - 1, 0), 1)

    @pl.when(jnp.logical_not(fast))
    def _():
        def one(item, carry):
            qb = plan[4 + kind, item]
            bias0 = jnp.where(plan[kind, 2 * item] < 0, LOW, 0.0).astype(jnp.float32)
            bias1 = jnp.where(plan[kind, 2 * item + 1] < 0, LOW, 0.0).astype(jnp.float32)
            for hp, s in enumerate(scores(item)):
                row = qb * pairs + hp
                s = jnp.concatenate([s[:BLOCK] + bias0, s[BLOCK:] + bias1], axis=0)
                m_old = m_ref[row]
                m_new = jnp.maximum(m_old, jnp.max(s, axis=0, keepdims=True))
                p = jnp.exp(s - m_new).astype(jnp.bfloat16)
                alpha = jnp.exp(m_old - m_new)
                pv = jnp.dot(values(item, hp), p, preferred_element_type=jnp.float32)
                acc[row, :64, :] = acc[row, :64, :] * alpha[:, :BLOCK] + pv[:64, :BLOCK]
                acc[row, 64:, :] = acc[row, 64:, :] * alpha[:, BLOCK:] + pv[64:BLOCK, BLOCK:]
                l_ref[row] = l_ref[row] * alpha + pv[BLOCK:BLOCK + 1, :]
                m_ref[row] = m_new
            return carry

        lax.fori_loop(0, 2 * count, one, 0)

    if kind != LAST:
        stores = [(acc, acc_out), (m_ref, m_out), (l_ref, l_out)]
        if kind == FIRST:
            stores += [(wvt, wvt_out), (qbd, qbd_out)]
        stores = [pltpu.make_async_copy(x, y, out_sem.at[i]) for i, (x, y) in enumerate(stores)]
        for store in stores:
            store.start()
        for store in stores:
            store.wait()
        if kind == FIRST:
            again.wait()

    if kind == LAST:
        @pl.loop(0, nqb)
        def _(qb):
            parts = []
            for hp in range(pairs):
                row = qb * pairs + hp
                inv = 1.0 / l_ref[row]
                parts.append(acc[row, :64, :] * inv[:, :BLOCK])
                parts.append(acc[row, 64:, :] * inv[:, BLOCK:])
            ctx = jnp.concatenate(parts, axis=0).T.astype(jnp.bfloat16)
            out[pl.ds(pl.multiple_of(qb * BLOCK, BLOCK), BLOCK), :] = cast_dot(ctx, wo[...], ((1,), (0,)))


def run_phase(kind, toks, wk, nbound, lists=None, wq=None, state=None, ends=None):
    width = wk.shape[0]
    pairs = width // BLOCK
    nkb = sum(t.shape[0] for t in toks) // BLOCK + (nbound // BLOCK if kind == LAST else 0)
    vmem, smem = pl.BlockSpec(memory_space=pltpu.VMEM), pl.BlockSpec(memory_space=pltpu.SMEM)
    hbm = pl.BlockSpec(memory_space=pltpu.HBM)
    if kind == FIRST:
        big, small = [wk, wq, *toks], list(lists)
        small_specs = [smem] * 3
        nqb = toks[0].shape[0] // BLOCK
    else:
        wvt, plan, qbd, *sums = state
        big, small = [wk, wvt, *toks, qbd, *sums], [plan]
        small_specs = [smem]
        nqb = qbd.shape[0]
    if kind == LAST:
        ids, gathered, wo = ends
        big += [gathered, wo]
        small.append(ids)
        small_specs.append(vmem)
    args, specs = big + small, [hbm] * len(big) + small_specs
    shapes = [(nqb * pairs, BLOCK, BLOCK), (nqb * pairs + 1, 1, 2 * BLOCK), (nqb * pairs, 1, 2 * BLOCK)]
    q_shape = (nqb, pairs, BLOCK, 2 * BLOCK)
    outs, out_specs = [], []
    scratch = [pltpu.VMEM(x.shape, x.dtype) for x in big]
    if kind == LAST:
        outs.append(jax.ShapeDtypeStruct((nqb * BLOCK, width), jnp.bfloat16))
        out_specs.append(vmem)
    else:
        if kind == FIRST:
            outs += [
                jax.ShapeDtypeStruct((width, width), jnp.bfloat16),
                jax.ShapeDtypeStruct((8, PLAN_LEN), jnp.int32),
                jax.ShapeDtypeStruct(q_shape, jnp.bfloat16),
                jax.ShapeDtypeStruct(toks[0].shape, jnp.bfloat16),
            ]
            out_specs += [hbm, smem, hbm, hbm]
            scratch += [pltpu.VMEM((width, width), jnp.bfloat16), pltpu.VMEM(q_shape, jnp.bfloat16)]
            scratch += [pltpu.VMEM(s, jnp.float32) for s in shapes]
        outs += [jax.ShapeDtypeStruct(s, jnp.float32) for s in shapes]
        out_specs += [hbm] * 3
    scratch += [
        pltpu.VMEM((nkb, BLOCK, width), jnp.bfloat16),
        pltpu.VMEM((nkb, width, BLOCK), jnp.bfloat16),
        pltpu.VMEM((2, pairs, 2 * BLOCK, 2 * BLOCK), jnp.bfloat16),
        pltpu.VMEM((1, BLOCK), jnp.float32),
    ]
    if kind == FIRST:
        scratch += [pltpu.VMEM((1, ROWS), jnp.float32), pltpu.VMEM((width, width), jnp.bfloat16)]
    if kind == LAST:
        scratch.append(pltpu.VMEM((nbound, width), jnp.bfloat16))
    scratch += [pltpu.SemaphoreType.DMA((len(big),)), pltpu.SemaphoreType.DMA((6,))]
    units = {FIRST: 18, MIDDLE: 34, LAST: 43}[kind]
    cost = pl.CostEstimate(
        flops=units * 8 * 2 * BLOCK ** 3 * 8 + nkb * BLOCK * width * width * 4,
        bytes_accessed=8 << 20,
        transcendentals=units * 8 * BLOCK * BLOCK,
    )
    return pl.pallas_call(
        functools.partial(phase, kind, len(toks), nbound),
        out_shape=outs,
        in_specs=specs,
        out_specs=out_specs,
        scratch_shapes=scratch,
        compiler_params=pltpu.CompilerParams(vmem_limit_bytes=63 << 20),
        cost_estimate=cost,
        name=("attend_own", "attend_middle", "attend_last")[kind],
    )(*args)


def send(value, pairs):
    return lax.ppermute(value, "curve", pairs)


def on_device(tokens, w_query, w_keyval, w_out, block_list, block_count, bnd_ids):
    tok_dev, width = tokens.shape
    nbound = bnd_ids.shape[0]
    size = lax.axis_size("curve")
    member = lax.axis_index("curve")
    everyone = range(size)

    vmem, smem = pl.BlockSpec(memory_space=pltpu.VMEM), pl.BlockSpec(memory_space=pltpu.SMEM)
    me = member.reshape(1).astype(jnp.int32)
    ids = bnd_ids.reshape(1, nbound)
    rows = pl.pallas_call(
        pick_rows,
        out_shape=jax.ShapeDtypeStruct((BCAP, width), jnp.bfloat16),
        in_specs=[smem, vmem, vmem],
        out_specs=vmem,
        compiler_params=pltpu.CompilerParams(vmem_limit_bytes=63 << 20),
        name="pick_rows",
    )(me, ids, tokens)
    gathered = lax.all_gather(rows, "curve", axis=0, tiled=True)

    from_two_behind = send(tokens, [(i, i + 2) for i in everyone if i + 2 < size])
    from_two_ahead = send(tokens, [(i, i - 2) for i in everyone if i >= 2])
    mate = send(tokens, [(i, i ^ 1) for i in everyone])

    wvt, plan, qbd, again, *sums = run_phase(
        FIRST, [tokens], w_keyval, nbound, lists=(me, block_list, block_count), wq=w_query
    )

    hops = [(i, i + 1 if i % 2 else i - 1) for i in everyone]
    far = send(again, [(a, b) for a, b in hops if 0 <= b < size])

    sums = run_phase(
        MIDDLE,
        [from_two_behind, from_two_ahead, mate],
        w_keyval,
        nbound,
        state=[wvt, plan, qbd, *sums],
    )
    (mixed,) = run_phase(
        LAST, [far], w_keyval, nbound, state=[wvt, plan, qbd, *sums], ends=(ids, gathered, w_out)
    )
    return mixed


def solution(mesh):
    in_specs = (
        P(("geo", "curve"), None),
        P(),
        P(),
        P(),
        P(("geo", "curve"), None),
        P(("geo", "curve")),
        P("geo"),
    )
    out_specs = P(("geo", "curve"), None)
    return jax.shard_map(
        on_device, mesh=mesh, in_specs=in_specs, out_specs=out_specs, check_vma=False
    )
```

```python
import functools

import jax
import jax.numpy as jnp
from jax import lax
from jax.experimental import pallas as pl
from jax.experimental.pallas import tpu as pltpu
from jax.sharding import PartitionSpec as P

HEADS = 8
BLOCK = 128
NB = 12
BCAP = 128
LOW = -1e30
ROWS = 256

FIRST, MIDDLE, LAST = range(3)
PLAN_LEN = 128


def cast_dot(a, b, dims):
    out = lax.dot_general(a, b, (dims, ((), ())), preferred_element_type=jnp.float32)
    return out.astype(jnp.bfloat16)


def project(tok, wk, wvt, k_ref, vt_ref, norm_ref, base):
    width = wvt.shape[0]
    feature = lax.broadcasted_iota(jnp.int32, (width, BLOCK), 0)
    head = lax.broadcasted_iota(jnp.int32, (width, BLOCK), 1)
    ind = jnp.where(feature >> 6 == head, 1.0, 0.0).astype(jnp.bfloat16)

    @pl.loop(0, tok.shape[0] // ROWS)
    def _(t):
        rows = tok[pl.ds(pl.multiple_of(t * ROWS, ROWS), ROWS), :]
        k = cast_dot(rows, wk[:, :width], ((1,), (0,)))
        vt = cast_dot(wvt[...], rows, ((1,), (1,)))
        for i in range(ROWS // BLOCK):
            at = base + t * (ROWS // BLOCK) + i
            k_ref[at] = k[i * BLOCK:(i + 1) * BLOCK, :]
            vt_ref[at] = vt[:, i * BLOCK:(i + 1) * BLOCK]
        norm = jnp.dot(k * k, ind, preferred_element_type=jnp.float32)
        norm_ref[...] = jnp.maximum(norm_ref[...], jnp.max(norm, axis=0, keepdims=True))


def plan_row(me, nqb, nbound, lists, counts, plan, qb, tops):
    used = counts[qb]
    near = 3 - 2 * lax.rem(me, 2)
    ns = list(tops)
    for i in range(NB):
        rel = jnp.clip(lists[qb, i] - (me - 2) * nqb, 0, 5 * nqb - 1)
        slot = lax.div(rel, nqb)
        src = jnp.where(slot == 4, 1, jnp.where(slot == near, 2, 0))
        block = src * nqb + rel - slot * nqb
        last = slot == 4 - near
        own = slot == 2
        live = (i < used).astype(jnp.int32)
        kind = jnp.where(own, FIRST, jnp.where(last, LAST, MIDDLE))
        for k in (FIRST, MIDDLE, LAST):
            plan[k, ns[k]] = block
            ns[k] = ns[k] + jnp.where(kind == k, live, 0)
    for k in (FIRST, MIDDLE, LAST):
        plan[k, ns[k]] = -1
        top = tops[k] + 2 * lax.div(ns[k] - tops[k] + 1, 2)
        if k == LAST:
            for j in range(nbound // BLOCK):
                plan[k, top + j] = nqb + j
            top = top + nbound // BLOCK
        first = lax.div(tops[k], 2)
        for j in range((NB + nbound // BLOCK) // 2 if k == LAST else NB // 2):
            plan[4 + k, first + j] = qb
        ns[k] = top
    return tuple(ns)


def plan_end(plan, tops):
    for k in (FIRST, MIDDLE, LAST):
        plan[k, tops[k]] = -1
        plan[k, tops[k] + 1] = -1
        plan[4 + k, lax.div(tops[k], 2)] = 0
        plan[7, k] = lax.div(tops[k] + 2, 4)


def pick_rows(me_ref, ids, tokens, out):
    me, tok_dev = me_ref[0], tokens.shape[0]
    n = ids.shape[1]
    mine = ids[...]
    start = jnp.sum(jnp.where(mine < me * tok_dev, 1.0, 0.0), axis=1, keepdims=True).astype(jnp.int32)
    r = lax.broadcasted_iota(jnp.int32, (BCAP, n), 0)
    j = lax.broadcasted_iota(jnp.int32, (BCAP, n), 1)
    local = (mine - me * tok_dev).astype(jnp.float32)
    spot = jnp.sum(jnp.where(j - r == start, local, 0.0), axis=1, keepdims=True).astype(jnp.int32)
    t = lax.broadcasted_iota(jnp.int32, (BCAP, tok_dev), 1)
    chosen = jnp.where(t == spot, 1.0, 0.0).astype(jnp.bfloat16)
    out[...] = cast_dot(chosen, tokens[...], ((1,), (0,)))


def join_rows(ids, gathered, out, tok_dev):
    n = ids.shape[1]
    size = gathered.shape[0] // BCAP
    mine = ids[...]
    j = lax.broadcasted_iota(jnp.int32, (n, BCAP), 0)
    r = lax.broadcasted_iota(jnp.int32, (n, BCAP), 1)
    starts = [
        jnp.sum(jnp.where(mine < o * tok_dev, 1.0, 0.0), axis=1, keepdims=True).astype(jnp.int32)
        for o in range(size + 1)
    ]
    parts = []
    for o in range(size):
        hit = jnp.logical_and(j - r == starts[o], r < starts[o + 1] - starts[o])
        parts.append(jnp.where(hit, 1.0, 0.0).astype(jnp.bfloat16))
    out[...] = cast_dot(jnp.concatenate(parts, axis=1), gathered[...], ((1,), (0,)))


def phase(kind, nsrc, nbound, *refs):
    refs = list(refs)
    take = lambda n: [refs.pop(0) for _ in range(n)]
    nin = nsrc + {FIRST: 2, MIDDLE: 6, LAST: 8}[kind]
    hbm_in = take(nin)
    if kind == FIRST:
        me_ref, lists, counts, _ = take(4)
    else:
        (plan,) = take(1)
    if kind == LAST:
        ids, out = take(2)
    else:
        if kind == FIRST:
            wvt_out, plan, qbd_out, tok_out = take(4)
        acc_out, m_out, l_out = take(3)
    bufs = take(nin)
    loads = []
    in_sem, out_sem = refs[-2:]
    for i in range(nin):
        loads.append(pltpu.make_async_copy(hbm_in[i], bufs[i], in_sem.at[i]))
        loads[i].start()
    wk, toks = bufs[0], bufs[2:2 + nsrc]
    if kind == FIRST:
        wq = bufs[1]
        wvt, qbd, acc, m_ref, l_ref = take(5)
    else:
        wvt, qbd = bufs[1], bufs[2 + nsrc]
        acc, m_ref, l_ref = bufs[3 + nsrc:6 + nsrc]
        if kind == LAST:
            gathered, wo = bufs[6 + nsrc:8 + nsrc]
    k_ref, vt_ref, p_ref, norm_ref = take(4)
    nqb, pairs = qbd.shape[0], qbd.shape[1]

    norm_ref[...] = jnp.zeros_like(norm_ref)
    if kind == FIRST:
        qn_ref, wqt = take(2)
        for load in loads:
            load.wait()
        again = pltpu.make_async_copy(toks[0], tok_out, out_sem.at[5])
        again.start()
        wqt[...] = wq[...].T
        wvt[...] = wk[:, wvt.shape[0]:].T
        qn_ref[...] = jnp.zeros_like(qn_ref)
        zero = jnp.zeros((64, BLOCK), jnp.bfloat16)

        def query(t, tops):
            rows = toks[0][pl.ds(pl.multiple_of(t * ROWS, ROWS), ROWS), :]
            q = lax.dot_general(wqt[...], rows, (((1,), (1,)), ((), ())), preferred_element_type=jnp.float32)
            q = q.astype(jnp.bfloat16) * jnp.bfloat16(0.125)
            for i in range(ROWS // BLOCK):
                for hp in range(pairs):
                    cut = q[hp * BLOCK:(hp + 1) * BLOCK, i * BLOCK:(i + 1) * BLOCK]
                    at = t * (ROWS // BLOCK) + i
                    qbd[at, hp, :64, :] = jnp.concatenate([cut[:64], zero], axis=1)
                    qbd[at, hp, 64:, :] = jnp.concatenate([zero, cut[64:]], axis=1)
            q = q.astype(jnp.float32)
            for h in range(2 * pairs):
                part = q[h * 64:(h + 1) * 64, :]
                qn_ref[...] = jnp.maximum(qn_ref[...], jnp.sum(part * part, axis=0, keepdims=True))
            for i in range(ROWS // BLOCK):
                qb = t * (ROWS // BLOCK) + i
                tops = plan_row(me_ref[0], nqb, nbound, lists, counts, plan, qb, tops)
            return tops

        tops = lax.fori_loop(0, toks[0].shape[0] // ROWS, query, (jnp.int32(0),) * 3)
        plan_end(plan, tops)
        acc[...] = jnp.zeros_like(acc)
        l_ref[...] = jnp.zeros_like(l_ref)
        qn = jnp.max(qn_ref[...])
    else:
        loads[0].wait()
        loads[1].wait()

    base = 0
    for i, tok in enumerate(toks):
        if kind != FIRST:
            loads[2 + i].wait()
        project(tok, wk, wvt, k_ref, vt_ref, norm_ref, base)
        base += tok.shape[0] // BLOCK
    if kind != FIRST:
        for load in loads[2 + nsrc:]:
            load.wait()
        qn = jnp.max(m_ref[nqb * pairs])
    if kind == LAST:
        (bound,) = take(1)
        join_rows(ids, gathered, bound, toks[0].shape[0])
        project(bound, wk, wvt, k_ref, vt_ref, norm_ref, base)
    fast = jnp.logical_and(qn < 1e20, qn * jnp.max(norm_ref[...]) <= 3600.0)
    if kind == FIRST:
        m_ref[...] = jnp.full_like(m_ref, jnp.where(fast, 0.0, LOW))
    m_ref[nqb * pairs] = jnp.full_like(m_ref[nqb * pairs], jnp.where(fast, qn, -LOW))
    count = plan[7, kind]

    def blocks(item):
        return jnp.maximum(plan[kind, 2 * item], 0), jnp.maximum(plan[kind, 2 * item + 1], 0)

    def scores(item):
        b0, b1 = blocks(item)
        qb = plan[4 + kind, item]
        made = []
        for hp in range(pairs):
            cut = slice(hp * BLOCK, (hp + 1) * BLOCK)
            k = jnp.concatenate([k_ref[b0, :, cut], k_ref[b1, :, cut]], axis=0)
            made.append(jnp.dot(k, qbd[qb, hp], preferred_element_type=jnp.float32))
        return made

    def values(item, hp):
        b0, b1 = blocks(item)
        cut = slice(hp * BLOCK, (hp + 1) * BLOCK)
        halves = []
        for b, live in ((b0, plan[kind, 2 * item] >= 0), (b1, plan[kind, 2 * item + 1] >= 0)):
            v = jnp.concatenate([vt_ref[b, cut, :], jnp.ones((16, BLOCK), jnp.bfloat16)], axis=0)
            halves.append(v * jnp.where(live, 1.0, 0.0).astype(jnp.bfloat16))
        return jnp.concatenate(halves, axis=1)

    @pl.when(fast)
    def _():
        def weigh(item, slot):
            for hp, s in enumerate(scores(item)):
                p_ref[slot, hp] = jnp.exp(s).astype(jnp.bfloat16)

        def gather(item, slot):
            qb = plan[4 + kind, item]
            pvs = [
                jnp.dot(values(item, hp), p_ref[slot, hp], preferred_element_type=jnp.float32)
                for hp in range(pairs)
            ]
            for hp, pv in enumerate(pvs):
                row = qb * pairs + hp
                acc[row, :64, :] = acc[row, :64, :] + pv[:64, :BLOCK]
                acc[row, 64:, :] = acc[row, 64:, :] + pv[64:BLOCK, BLOCK:]
                l_ref[row] = l_ref[row] + pv[BLOCK:BLOCK + 1, :]

        p_ref[1] = jnp.zeros_like(p_ref[1])

        def two(t, carry):
            gather(jnp.maximum(2 * t - 1, 0), 1)
            weigh(2 * t, 0)
            gather(2 * t, 0)
            weigh(2 * t + 1, 1)
            return carry

        lax.fori_loop(0, count, two, 0)
        gather(jnp.maximum(2 * count - 1, 0), 1)

    @pl.when(jnp.logical_not(fast))
    def _():
        def one(item, carry):
            qb = plan[4 + kind, item]
            bias0 = jnp.where(plan[kind, 2 * item] < 0, LOW, 0.0).astype(jnp.float32)
            bias1 = jnp.where(plan[kind, 2 * item + 1] < 0, LOW, 0.0).astype(jnp.float32)
            for hp, s in enumerate(scores(item)):
                row = qb * pairs + hp
                s = jnp.concatenate([s[:BLOCK] + bias0, s[BLOCK:] + bias1], axis=0)
                m_old = m_ref[row]
                m_new = jnp.maximum(m_old, jnp.max(s, axis=0, keepdims=True))
                p = jnp.exp(s - m_new).astype(jnp.bfloat16)
                alpha = jnp.exp(m_old - m_new)
                pv = jnp.dot(values(item, hp), p, preferred_element_type=jnp.float32)
                acc[row, :64, :] = acc[row, :64, :] * alpha[:, :BLOCK] + pv[:64, :BLOCK]
                acc[row, 64:, :] = acc[row, 64:, :] * alpha[:, BLOCK:] + pv[64:BLOCK, BLOCK:]
                l_ref[row] = l_ref[row] * alpha + pv[BLOCK:BLOCK + 1, :]
                m_ref[row] = m_new
            return carry

        lax.fori_loop(0, 2 * count, one, 0)

    if kind != LAST:
        stores = [(acc, acc_out), (m_ref, m_out), (l_ref, l_out)]
        if kind == FIRST:
            stores += [(wvt, wvt_out), (qbd, qbd_out)]
        stores = [pltpu.make_async_copy(x, y, out_sem.at[i]) for i, (x, y) in enumerate(stores)]
        for store in stores:
            store.start()
        for store in stores:
            store.wait()
        if kind == FIRST:
            again.wait()

    if kind == LAST:
        @pl.loop(0, nqb)
        def _(qb):
            parts = []
            for hp in range(pairs):
                row = qb * pairs + hp
                inv = 1.0 / l_ref[row]
                parts.append(acc[row, :64, :] * inv[:, :BLOCK])
                parts.append(acc[row, 64:, :] * inv[:, BLOCK:])
            ctx = jnp.concatenate(parts, axis=0).T.astype(jnp.bfloat16)
            out[pl.ds(pl.multiple_of(qb * BLOCK, BLOCK), BLOCK), :] = cast_dot(ctx, wo[...], ((1,), (0,)))


def run_phase(kind, toks, wk, nbound, lists=None, wq=None, state=None, ends=None):
    width = wk.shape[0]
    pairs = width // BLOCK
    nkb = sum(t.shape[0] for t in toks) // BLOCK + (nbound // BLOCK if kind == LAST else 0)
    vmem, smem = pl.BlockSpec(memory_space=pltpu.VMEM), pl.BlockSpec(memory_space=pltpu.SMEM)
    hbm = pl.BlockSpec(memory_space=pltpu.HBM)
    if kind == FIRST:
        big, small = [wk, wq, *toks], list(lists)
        small_specs = [smem] * 3 + [hbm]
        nqb = toks[0].shape[0] // BLOCK
    else:
        wvt, plan, qbd, *sums = state
        big, small = [wk, wvt, *toks, qbd, *sums], [plan]
        small_specs = [smem]
        nqb = qbd.shape[0]
    if kind == LAST:
        ids, gathered, wo = ends
        big += [gathered, wo]
        small.append(ids)
        small_specs.append(vmem)
    args, specs = big + small, [hbm] * len(big) + small_specs
    shapes = [(nqb * pairs, BLOCK, BLOCK), (nqb * pairs + 1, 1, 2 * BLOCK), (nqb * pairs, 1, 2 * BLOCK)]
    q_shape = (nqb, pairs, BLOCK, 2 * BLOCK)
    outs, out_specs = [], []
    scratch = [pltpu.VMEM(x.shape, x.dtype) for x in big]
    if kind == LAST:
        outs.append(jax.ShapeDtypeStruct((nqb * BLOCK, width), jnp.bfloat16))
        out_specs.append(vmem)
    else:
        if kind == FIRST:
            outs += [
                jax.ShapeDtypeStruct((width, width), jnp.bfloat16),
                jax.ShapeDtypeStruct((8, PLAN_LEN), jnp.int32),
                jax.ShapeDtypeStruct(q_shape, jnp.bfloat16),
                jax.ShapeDtypeStruct(toks[0].shape, jnp.bfloat16),
            ]
            out_specs += [hbm, smem, hbm, hbm]
            scratch += [pltpu.VMEM((width, width), jnp.bfloat16), pltpu.VMEM(q_shape, jnp.bfloat16)]
            scratch += [pltpu.VMEM(s, jnp.float32) for s in shapes]
        outs += [jax.ShapeDtypeStruct(s, jnp.float32) for s in shapes]
        out_specs += [hbm] * 3
    scratch += [
        pltpu.VMEM((nkb, BLOCK, width), jnp.bfloat16),
        pltpu.VMEM((nkb, width, BLOCK), jnp.bfloat16),
        pltpu.VMEM((2, pairs, 2 * BLOCK, 2 * BLOCK), jnp.bfloat16),
        pltpu.VMEM((1, BLOCK), jnp.float32),
    ]
    if kind == FIRST:
        scratch += [pltpu.VMEM((1, ROWS), jnp.float32), pltpu.VMEM((width, width), jnp.bfloat16)]
    if kind == LAST:
        scratch.append(pltpu.VMEM((nbound, width), jnp.bfloat16))
    scratch += [pltpu.SemaphoreType.DMA((len(big),)), pltpu.SemaphoreType.DMA((6,))]
    units = {FIRST: 18, MIDDLE: 34, LAST: 43}[kind]
    cost = pl.CostEstimate(
        flops=units * 8 * 2 * BLOCK ** 3 * 8 + nkb * BLOCK * width * width * 4,
        bytes_accessed=8 << 20,
        transcendentals=units * 8 * BLOCK * BLOCK,
    )
    return pl.pallas_call(
        functools.partial(phase, kind, len(toks), nbound),
        out_shape=outs,
        in_specs=specs,
        out_specs=out_specs,
        scratch_shapes=scratch,
        compiler_params=pltpu.CompilerParams(vmem_limit_bytes=63 << 20),
        cost_estimate=cost,
        name=("attend_own", "attend_middle", "attend_last")[kind],
    )(*args)


def send(value, pairs):
    return lax.ppermute(value, "curve", pairs)


def on_device(tokens, w_query, w_keyval, w_out, block_list, block_count, bnd_ids):
    tok_dev, width = tokens.shape
    nbound = bnd_ids.shape[0]
    size = lax.axis_size("curve")
    member = lax.axis_index("curve")
    everyone = range(size)

    vmem, smem = pl.BlockSpec(memory_space=pltpu.VMEM), pl.BlockSpec(memory_space=pltpu.SMEM)
    me = member.reshape(1).astype(jnp.int32)
    ids = bnd_ids.reshape(1, nbound)
    rows = pl.pallas_call(
        pick_rows,
        out_shape=jax.ShapeDtypeStruct((BCAP, width), jnp.bfloat16),
        in_specs=[smem, vmem, vmem],
        out_specs=vmem,
        compiler_params=pltpu.CompilerParams(vmem_limit_bytes=63 << 20),
        name="pick_rows",
    )(me, ids, tokens)
    gathered = lax.all_gather(rows, "curve", axis=0, tiled=True)

    from_two_behind = send(tokens, [(i, i + 2) for i in everyone if i + 2 < size])
    from_two_ahead = send(tokens, [(i, i - 2) for i in everyone if i >= 2])
    mate = send(tokens, [(i, i ^ 1) for i in everyone])

    wvt, plan, qbd, again, *sums = run_phase(
        FIRST, [tokens], w_keyval, nbound, lists=(me, block_list, block_count, rows), wq=w_query
    )

    hops = [(i, i + 1 if i % 2 else i - 1) for i in everyone]
    far = send(again, [(a, b) for a, b in hops if 0 <= b < size])

    sums = run_phase(
        MIDDLE,
        [from_two_behind, from_two_ahead, mate],
        w_keyval,
        nbound,
        state=[wvt, plan, qbd, *sums],
    )
    (mixed,) = run_phase(
        LAST, [far], w_keyval, nbound, state=[wvt, plan, qbd, *sums], ends=(ids, gathered, w_out)
    )
    return mixed


def solution(mesh):
    in_specs = (
        P(("geo", "curve"), None),
        P(),
        P(),
        P(),
        P(("geo", "curve"), None),
        P(("geo", "curve")),
        P("geo"),
    )
    out_specs = P(("geo", "curve"), None)
    return jax.shard_map(
        on_device, mesh=mesh, in_specs=in_specs, out_specs=out_specs, check_vma=False
    )
```
